32 devices in a mesh: groups: 2 (over x), tm: 16 (over z, y, core).
Axes of the slice: x: 2, y: 2, z: 4, core: 2. Of those that a mesh axis runs over, the one named last changes fastest.
Arguments:
- tokens: bfloat16 [4096, 1536], P(('groups', 'tm')), parts along dimension 0, may hold values from -6 to 6
- target: bfloat16 [4096, 1536], P(('groups', 'tm')), parts along dimension 0, may hold values from -3 to 3
- w_query: bfloat16 [1536, 1536], P('tm'), may hold values from -0.15625 to 0.15625
- w_key: bfloat16 [1536, 1536], P('tm'), may hold values from -0.15625 to 0.15625
- w_value: bfloat16 [1536, 1536], P('tm'), may hold values from -0.15625 to 0.15625
- q_gain: float32 [128], replicated, may hold values from 0.5 to 2
- k_gain: float32 [128], replicated, may hold values from 0.5 to 2
- block_weight: float32 [16], P('groups'), parts along dimension 0
- block_reset: int32 [16], P('groups'), parts along dimension 0, may hold values 0 or 1
- valid_count: int32 [16], P('groups'), parts along dimension 0, may hold values from 192 to 256
Outputs:
- input_grad: bfloat16 [4096, 1536], P(('groups', 'tm')), parts along dimension 0
- loss: float32 [2], P('groups'), parts along dimension 0
The draws below stay inside these ranges and needn't reach their ends.
There are 2 independent parts, one for each index of `groups`. The reference program is written for one: setup_inputs(seed, part) draws one part's arguments, and reference() takes and returns one part's arrays. A program takes and returns all parts, laid end to end along the dimension named above; an argument that names none is the same for every part. Nothing has to cross between parts.
All inputs are finite; a program needn't handle non-finite values.
Results may differ from the reference program's by a relative error of at most 0.012.
The reference program's roundings to bfloat16 on the way (of `value_cast`, `probs_cast`, `attended`, `attended_grad`, `score_grad` and `value_total`) count: a program that leaves them out, or rounds other values in their place, can miss the bound.
Values may be sent and summed in bfloat16 or wider, within the bound.
A program may use at most 128 MiB of HBM per device.

```python
import math
import jax
import jax.numpy as jnp
from jax import lax

D = 1536
HEADS = 12
HEAD = 128
BLOCK = 256
WIDTH = 1536
BLOCKS = 8
TOKENS = 2048


def draw_block_weight(key, part):
    place = jnp.arange(BLOCKS, dtype=jnp.float32) / max(BLOCKS - 1, 1)
    rise = jnp.exp(place * math.log(3.0))
    noise = jnp.exp(jax.random.uniform(key, (BLOCKS,), jnp.float32, -0.35, 0.35))
    return (0.5 * rise * noise).astype(jnp.float32)


def with_ends(drawn, key, smallest, high):
    index_at = [jax.random.randint(jax.random.fold_in(key, axis), (), 0, length) for axis, length in enumerate(drawn.shape)]
    widest = drawn.shape.index(max(drawn.shape))
    neighbour = index_at[:widest] + [(index_at[widest] + 1) % drawn.shape[widest]] + index_at[widest + 1:]
    return drawn.at[tuple(index_at)].set(smallest).at[tuple(neighbour)].set(high)


def levels(rng, extent, cuts, least, largest):
    level, own = 1.0, jax.random.fold_in(rng, 6)
    for position, shards_of in cuts:
        steps = jnp.exp(jax.random.uniform(jax.random.fold_in(own, position), (shards_of,), jnp.float32, least / len(cuts), largest / len(cuts)))
        level = level * jnp.repeat(steps, extent[position] // shards_of).reshape([-1 if axis == position else 1 for axis in range(len(extent))])
    return level


def gaussian(rng, dims, deviation, reach, split=(), kind=jnp.bfloat16):
    values = jax.random.normal(rng, dims, jnp.float32) * deviation
    if len(split) > 0:
        values = levels(rng, dims, split, -0.22, 0.18) * values
    return jnp.clip(values, min=-reach, max=reach).astype(kind)


def setup_inputs(seed: int = 0, part: int = 0) -> dict:
    keys = jax.random.split(jax.random.key(seed), 11)
    part_keys = jax.random.split(jax.random.fold_in(keys[10], part), 11)
    return {
        "tokens": gaussian(part_keys[0], (TOKENS, D), 1.0, 6.0, ((0, 16),)),
        "target": gaussian(part_keys[1], (TOKENS, WIDTH), 0.5, 3.0, ((0, 16),)),
        "w_query": gaussian(keys[2], (D, WIDTH), D ** -0.5, 0.15625, ((0, 16),)),
        "w_key": gaussian(keys[3], (D, WIDTH), D ** -0.5, 0.15625, ((0, 16),)),
        "w_value": gaussian(keys[4], (D, WIDTH), D ** -0.5, 0.15625, ((0, 16),)),
        "q_gain": jnp.clip(jnp.exp(jax.random.uniform(keys[5], (HEAD,), jnp.float32, math.log(0.5), math.log(2.0))), 0.5, 2.0),
        "k_gain": jnp.clip(jnp.exp(jax.random.uniform(keys[6], (HEAD,), jnp.float32, math.log(0.5), math.log(2.0))), 0.5, 2.0),
        "block_weight": draw_block_weight(jax.random.fold_in(jax.random.fold_in(keys[10], part), 71), part),
        "block_reset": with_ends((jax.random.randint(part_keys[8], (BLOCKS,), 0, 8) < 1).astype(jnp.int32), jax.random.fold_in(part_keys[8], 1), 0, 1),
        "valid_count": with_ends(jax.random.randint(part_keys[9], (BLOCKS,), BLOCK - BLOCK // 4, BLOCK + 1), jax.random.fold_in(part_keys[9], 1), BLOCK - BLOCK // 4, BLOCK).astype(jnp.int32),
    }


epsilon = 1e-06
loss_scale = 32.0
group_heads = 4

def unit_heads(values, head_size):
    shaped = values.reshape(values.shape[0], values.shape[1] // head_size, head_size)
    factor = lax.rsqrt(lax.optimization_barrier(jnp.mean(shaped * shaped, axis=-1, keepdims=True)) + epsilon)
    return (shaped * factor, factor)

def norm_backward(upstream, unit, factor, gain):
    shaped = upstream.reshape(unit.shape) * gain
    result = factor * (shaped - unit * lax.optimization_barrier(jnp.mean(shaped * unit, axis=-1, keepdims=True)))
    return result.reshape(upstream.shape)

def group_pass(query_part, key_part, value_part, allowed, row_weight, target_part, head_size):
    query_rows = query_part.shape[0]
    key_rows = key_part.shape[0]
    heads = query_part.shape[1] // head_size
    query_heads = query_part.reshape(query_rows, heads, head_size).astype(jnp.float32)
    key_heads = key_part.reshape(key_rows, heads, head_size).astype(jnp.float32)
    value_heads = value_part.reshape(key_rows, heads, head_size).astype(jnp.float32)
    scores = jnp.einsum('qhd,khd->hqk', query_heads, key_heads) / math.sqrt(head_size)
    expo = jnp.where(allowed[None], jnp.exp(scores), jnp.zeros_like(scores))
    probs = expo / lax.optimization_barrier(jnp.sum(expo, axis=-1, keepdims=True))
    probs_cast = probs.astype(jnp.bfloat16)
    probs_wide = probs_cast.astype(jnp.float32)
    attended = jnp.einsum('hqk,khd->qhd', probs_wide, value_heads)
    attended = attended.reshape(query_rows, heads * head_size).astype(jnp.bfloat16)
    diff = attended.astype(jnp.float32) - target_part.astype(jnp.float32)
    loss_part = jnp.sum(row_weight[:, None] * diff * diff)
    attended_grad = (loss_scale * row_weight[:, None] * diff).astype(jnp.bfloat16)
    grad_heads = attended_grad.reshape(query_rows, heads, head_size).astype(jnp.float32)
    prob_grad = jnp.einsum('qhd,khd->hqk', grad_heads, value_heads)
    delta = lax.optimization_barrier(jnp.sum(probs * prob_grad, axis=-1, keepdims=True))
    score_grad = (probs * (prob_grad - delta) / math.sqrt(head_size)).astype(jnp.bfloat16)
    score_wide = score_grad.astype(jnp.float32)
    value_grad = jnp.einsum('hqk,qhd->khd', probs_wide, grad_heads).reshape(key_rows, heads * head_size)
    query_grad = jnp.einsum('hqk,khd->qhd', score_wide, key_heads).reshape(query_rows, heads * head_size)
    key_grad = jnp.einsum('hqk,qhd->khd', score_wide, query_heads).reshape(key_rows, heads * head_size)
    return (loss_part, query_grad, key_grad, value_grad)

def back_project(grad, weight):
    return lax.dot_general(grad, weight, (((1,), (1,)), ((), ())), preferred_element_type=jnp.float32)

def reference(tokens, target, w_query, w_key, w_value, q_gain, k_gain, block_weight, block_reset, valid_count):
    width = HEADS * HEAD
    queries_raw = jnp.dot(tokens, w_query, preferred_element_type=jnp.float32)
    keys_raw = jnp.dot(tokens, w_key, preferred_element_type=jnp.float32)
    values_raw = jnp.dot(tokens, w_value, preferred_element_type=jnp.float32)
    query_unit, query_factor = unit_heads(queries_raw, HEAD)
    key_unit, key_factor = unit_heads(keys_raw, HEAD)
    query_normed = (query_unit * q_gain).reshape(TOKENS, width).astype(jnp.bfloat16)
    key_normed = (key_unit * k_gain).reshape(TOKENS, width).astype(jnp.bfloat16)
    value_cast = values_raw.astype(jnp.bfloat16)
    key_blocks = key_normed.reshape(BLOCKS, BLOCK, width)
    value_blocks = value_cast.reshape(BLOCKS, BLOCK, width)
    empty = jnp.zeros((1, BLOCK, width), jnp.bfloat16)
    key_before = jnp.concatenate([empty, key_blocks[:-1]], axis=0)
    value_before = jnp.concatenate([empty, value_blocks[:-1]], axis=0)
    query_blocks = query_normed.reshape(BLOCKS, BLOCK, width)
    target_blocks = target.reshape(BLOCKS, BLOCK, width)

    def one_block(items):
        index, query_rows, key_prior, key_own, value_prior, value_own, target_rows = items
        own_count = valid_count[index]
        prior_count = jnp.where(index > 0, valid_count[jnp.maximum(index - 1, 0)], 0)
        reset_flag = block_reset[index]
        key_place = jnp.arange(2 * BLOCK, dtype=jnp.int32)
        in_own = key_place >= BLOCK
        key_pos = key_place % BLOCK
        limit = jnp.where(in_own, own_count, prior_count)
        allowed = (key_pos < limit) & (in_own | (index > 0) & (reset_flag == 0))
        query_pos = jnp.arange(BLOCK, dtype=jnp.int32)
        row_weight = jnp.where(query_pos < own_count, block_weight[index], 0.0).astype(jnp.float32)
        all_keys = jnp.concatenate([key_prior, key_own], axis=0)
        all_values = jnp.concatenate([value_prior, value_own], axis=0)
        group_width = group_heads * HEAD
        loss_part = jnp.zeros((), jnp.float32)
        query_grads, key_grads, value_grads = ([], [], [])
        for group in range(width // group_width):
            cols = slice(group * group_width, (group + 1) * group_width)
            part_loss, query_grad, key_grad, value_grad = group_pass(query_rows[:, cols], all_keys[:, cols], all_values[:, cols], allowed, row_weight, target_rows[:, cols], HEAD)
            loss_part = loss_part + part_loss
            query_grads.append(query_grad)
            key_grads.append(key_grad)
            value_grads.append(value_grad)
        return (loss_part, jnp.concatenate(query_grads, axis=1), jnp.concatenate(key_grads, axis=1), jnp.concatenate(value_grads, axis=1))
    loss_parts, query_grad, key_grad, value_grad = lax.map(one_block, (jnp.arange(BLOCKS, dtype=jnp.int32), query_blocks, key_before, key_blocks, value_before, value_blocks, target_blocks))
    zero_rows = jnp.zeros((1, BLOCK, width), jnp.float32)
    key_total = key_grad[:, BLOCK:] + jnp.concatenate([key_grad[1:, :BLOCK], zero_rows], axis=0)
    value_total = value_grad[:, BLOCK:] + jnp.concatenate([value_grad[1:, :BLOCK], zero_rows], axis=0)
    query_back = norm_backward(query_grad.reshape(TOKENS, width), query_unit, query_factor, q_gain).astype(jnp.bfloat16)
    key_back = norm_backward(key_total.reshape(TOKENS, width), key_unit, key_factor, k_gain).astype(jnp.bfloat16)
    value_back = value_total.reshape(TOKENS, width).astype(jnp.bfloat16)
    input_grad = back_project(query_back, w_query) + back_project(key_back, w_key) + back_project(value_back, w_value)
    loss = jnp.sum(loss_parts) / (TOKENS * width)
    return (input_grad.astype(jnp.bfloat16), loss.reshape(1))
```

```python
import functools
import math

import jax
import jax.numpy as jnp
from jax import lax
from jax.experimental import pallas as pl
from jax.experimental.pallas import tpu as pltpu
from jax.sharding import PartitionSpec as P

epsilon = 1e-06
loss_scale = 32.0
QUAD = 4
MESH = pl.DeviceIdType.MESH
ORDER = (1, 2, 0)


def gather_kernel(
    nz, tok, tgt, wq, wk, wv, tokb, tgtb, wbuf,
    inj_recv, inj_send, inj_local,
    up_recv, up_send, dn_recv, dn_send, x_recv, x_send,
    tok_recv, tok_send, tok_local, tgt_recv, tgt_send, tgt_local,
):
    g, t = lax.axis_index("groups"), lax.axis_index("tm")
    z, k = t // QUAD, t % QUAD
    y, c = k // 2, k % 2
    part = wbuf.shape[3]
    weights = (wq, wk, wv)
    has_up, has_dn = z + 1 < nz, z > 0
    ynbr = (g, t + 2 - 4 * y)
    cnbr = (g, t + 1 - 2 * c)
    xnbr = (g + 1 - 2 * (g % 2), t)
    half = g % 2

    barrier = pltpu.get_barrier_semaphore()

    def greet(device):
        pl.semaphore_signal(barrier, inc=1, device_id=device, device_id_type=MESH)

    for d in range(1, QUAD):
        greet((g, QUAD * z + (k + d) % QUAD))
    greet(xnbr)

    @pl.when(has_up)
    def _():
        for m in range(QUAD):
            greet((g, QUAD * (z + 1) + m))

    @pl.when(has_dn)
    def _():
        for m in range(QUAD):
            greet((g, QUAD * (z - 1) + m))

    sides = jnp.where(has_up, 1, 0) + jnp.where(has_dn, 1, 0)
    pl.semaphore_wait(barrier, QUAD + QUAD * sides)

    def remote(src, dst, send_sem, recv_sem, device):
        return pltpu.make_async_remote_copy(
            src_ref=src, dst_ref=dst, send_sem=send_sem, recv_sem=recv_sem,
            device_id=device, device_id_type=MESH,
        )

    def columns(ref, m):
        return ref.at[:, pl.ds(pl.multiple_of(m * part, 128), part)]

    def inject(w, d):
        m = (k + d) % QUAD
        return remote(
            columns(weights[w], m), wbuf.at[w, t], inj_send.at[w, d - 1], inj_recv.at[w, k],
            (g, QUAD * z + m),
        )

    def injected(w, d):
        m = (k + d) % QUAD
        slot = wbuf.at[w, QUAD * z + m]
        return remote(slot, slot, inj_send.at[w, d - 1], inj_recv.at[w, m], (g, QUAD * z + m))

    def inject_own(w):
        return pltpu.make_async_copy(columns(weights[w], k), wbuf.at[w, t], inj_local.at[w])

    def piece(w, q, h):
        return wbuf.at[w, pl.ds(QUAD * q + 2 * h, 2)]

    def go_up(w, q):
        return remote(
            piece(w, q, half), piece(w, q, half), up_send.at[w, q], up_recv.at[w, q], (g, t + QUAD)
        )

    def go_dn(w, q):
        return remote(
            piece(w, q, half), piece(w, q, half), dn_send.at[w, q], dn_recv.at[w, q], (g, t - QUAD)
        )

    def go_x(w, q):
        return remote(
            piece(w, q, half), piece(w, q, half), x_send.at[w, q], x_recv.at[w, q], xnbr
        )

    def from_x(w, q):
        return remote(
            piece(w, q, 1 - half), piece(w, q, 1 - half), x_send.at[w, q], x_recv.at[w, q], xnbr
        )

    own_slot = 2 * (1 + y) + c
    their_slot = 2 * (2 - y) + c
    halo_slot = 6 * (1 - y) + c
    their_halo = 6 * y + c
    has_halo = jnp.where(y == 1, z, nz - 1 - z) > 0
    has_their_halo = jnp.where(y == 0, z, nz - 1 - z) > 0
    give_halo = jnp.where(y == 0, z, nz - 1 - z) > 0
    halo_to = (g, jnp.where(y == 0, t - QUAD, t + QUAD))
    halo_to_slot = 6 * (1 - y) + c

    def send_tok(src, slot, i, device):
        return remote(src, tokb.at[slot], tok_send.at[i], tok_recv.at[slot], device)

    own_y = send_tok(tok, own_slot, 0, ynbr)
    own_c = send_tok(tok, own_slot, 1, cnbr)
    own_z = send_tok(tok, halo_to_slot, 2, halo_to)
    halo_y = send_tok(tokb.at[halo_slot], halo_slot, 3, ynbr)
    halo_c = send_tok(tokb.at[halo_slot], halo_slot, 4, cnbr)
    their_c = send_tok(tokb.at[their_slot], their_slot, 5, cnbr)
    their_halo_c = send_tok(tokb.at[their_halo], their_halo, 6, cnbr)
    tok_own = pltpu.make_async_copy(tok, tokb.at[own_slot], tok_local.at[0])

    def tok_wait(slot):
        send_tok(tokb.at[slot], slot, 0, cnbr).wait_recv()

    def tgt_quad(d):
        m = (k + d) % QUAD
        return remote(
            columns(tgt, m), tgtb.at[k], tgt_send.at[d - 1], tgt_recv.at[k], (g, QUAD * z + m)
        )

    def tgt_before(m):
        return remote(
            columns(tgt, m), tgtb.at[QUAD + c], tgt_send.at[3 + m], tgt_recv.at[QUAD + c],
            (g, QUAD * (z - 1) + m),
        )

    tgt_own = pltpu.make_async_copy(columns(tgt, k), tgtb.at[k], tgt_local.at[0])

    def tgt_wait(slot):
        remote(
            tgtb.at[slot], tgtb.at[slot], tgt_send.at[0], tgt_recv.at[slot], cnbr
        ).wait_recv()

    gives_target = jnp.where(y == 0, z, 0) > 0

    for w in ORDER:
        for d in (2, 3, 1):
            inject(w, d).start()
        inject_own(w).start()
        if w == ORDER[0]:

            @pl.when(give_halo)
            def _():
                own_z.start()

            own_y.start()
            own_c.start()
            tok_own.start()
    for d in range(1, QUAD):
        tgt_quad(d).start()
    tgt_own.start()

    @pl.when(gives_target)
    def _():
        for m in range(QUAD):
            tgt_before(m).start()

    for w in ORDER:
        for d in range(1, QUAD):
            injected(w, d).wait_recv()
        inject_own(w).wait()

        @pl.when(has_up)
        def _():
            go_up(w, z).start()

        @pl.when(has_dn)
        def _():
            go_dn(w, z).start()

    tok_wait(their_slot)
    their_c.start()

    @pl.when(has_halo)
    def _():
        tok_wait(halo_slot)
        halo_y.start()
        halo_c.start()

    for s in range(1, nz):
        for w in ORDER:

            @pl.when(z - s >= 0)
            def _():
                go_up(w, z - s).wait_recv()
                go_x(w, z - s).start()

                @pl.when(has_up)
                def _():
                    go_up(w, z - s).start()

            @pl.when(z + s < nz)
            def _():
                go_dn(w, z + s).wait_recv()
                go_x(w, z + s).start()

                @pl.when(has_dn)
                def _():
                    go_dn(w, z + s).start()

        if s == 1:

            @pl.when(has_their_halo)
            def _():
                tok_wait(their_halo)
                their_halo_c.start()

    other = 1 - 2 * c
    tok_wait(2 + c + other)
    tok_wait(4 + c + other)

    @pl.when(has_dn)
    def _():
        tok_wait(c + other)

    @pl.when(has_up)
    def _():
        tok_wait(6 + c + other)

    for d in range(1, QUAD):
        tgt_wait((k + d) % QUAD)

    @pl.when(has_up)
    def _():
        tgt_wait(QUAD)
        tgt_wait(QUAD + 1)

    for s in range(1, nz):
        for w in ORDER:

            @pl.when(z - s >= 0)
            def _():
                from_x(w, z - s).wait_recv()

            @pl.when(z + s < nz)
            def _():
                from_x(w, z + s).wait_recv()

    tok_own.wait()
    tgt_own.wait()
    own_y.wait_send()
    own_c.wait_send()
    their_c.wait_send()

    @pl.when(give_halo)
    def _():
        own_z.wait_send()

    @pl.when(has_halo)
    def _():
        halo_y.wait_send()
        halo_c.wait_send()

    @pl.when(has_their_halo)
    def _():
        their_halo_c.wait_send()

    for d in range(1, QUAD):
        tgt_quad(d).wait_send()

    @pl.when(gives_target)
    def _():
        for m in range(QUAD):
            tgt_before(m).wait_send()

    for w in ORDER:
        for d in range(1, QUAD):
            inject(w, d).wait_send()

        @pl.when(has_up)
        def _():
            go_up(w, z).wait_send()

        @pl.when(has_dn)
        def _():
            go_dn(w, z).wait_send()

        for s in range(1, nz):

            @pl.when(z - s >= 0)
            def _():
                go_x(w, z - s).wait_send()

                @pl.when(has_up)
                def _():
                    go_up(w, z - s).wait_send()

            @pl.when(z + s < nz)
            def _():
                go_x(w, z + s).wait_send()

                @pl.when(has_dn)
                def _():
                    go_dn(w, z + s).wait_send()


def gather(tokens, target, w_query, w_key, w_value, n):
    nz = n // QUAD
    rows, width = tokens.shape
    depth = w_query.shape[0]
    part = w_query.shape[1] // QUAD
    dma = pltpu.SemaphoreType.DMA
    any_spec = pl.BlockSpec(memory_space=pl.ANY)
    return pl.pallas_call(
        functools.partial(gather_kernel, nz),
        out_shape=(
            jax.ShapeDtypeStruct((8, rows, width), jnp.bfloat16),
            jax.ShapeDtypeStruct((6, rows, part), jnp.bfloat16),
            jax.ShapeDtypeStruct((3, n, depth, part), jnp.bfloat16),
        ),
        in_specs=[any_spec] * 5,
        out_specs=(any_spec,) * 3,
        scratch_shapes=[
            dma((3, QUAD)), dma((3, QUAD - 1)), dma((3,)),
            dma((3, nz)), dma((3, nz)), dma((3, nz)), dma((3, nz)), dma((3, nz)), dma((3, nz)),
            dma((8,)), dma((7,)), dma((1,)), dma((6,)), dma((7,)), dma((1,)),
        ],
        compiler_params=pltpu.CompilerParams(collective_id=0, has_side_effects=True),
    )(tokens, target, w_query, w_key, w_value)


def layer_kernel(
    heads, head_size, block,
    info, weight, tok, tgt, w, qg, kg, out, loss,
    raw_q, raw_k, qn, kn, vn, dq, dk, dv, back,
):
    scale = 1.0 / math.sqrt(head_size)
    q_gain, k_gain = qg[...], kg[...]
    f32, bf16 = jnp.float32, jnp.bfloat16

    def normed(raw, gain):
        factor = lax.rsqrt(jnp.mean(raw * raw, axis=-1, keepdims=True) + epsilon)
        return (raw * factor * gain).astype(bf16)

    for b in range(4):
        rows = slice(b * block, (b + 1) * block)
        x = tok[rows, :]
        if b == 0:
            x = jnp.where(info[7] > 0, x, jnp.zeros_like(x))
        if b == 3:
            x = jnp.where(info[8] > 0, x, jnp.zeros_like(x))
        keys = jnp.dot(x, w[1], preferred_element_type=f32)
        values = jnp.dot(x, w[2], preferred_element_type=f32)
        if b > 0:
            queries = jnp.dot(x, w[0], preferred_element_type=f32)
        for h in range(heads):
            cols = slice(h * head_size, (h + 1) * head_size)
            kn[h, rows, :] = normed(keys[:, cols], k_gain)
            vn[h, rows, :] = values[:, cols].astype(bf16)
            if b > 0:
                qn[h, (b - 1) * block : b * block, :] = normed(queries[:, cols], q_gain)
            if b == 1 or b == 2:
                own = slice((b - 1) * block, b * block)
                raw_k[h, own, :] = keys[:, cols]
                raw_q[h, own, :] = queries[:, cols]

    dk[...] = jnp.zeros_like(dk)
    dv[...] = jnp.zeros_like(dv)
    loss[...] = jnp.zeros_like(loss)

    key_place = lax.broadcasted_iota(jnp.int32, (1, 2 * block), 1)
    in_own = key_place >= block
    key_pos = jnp.where(in_own, key_place - block, key_place)
    query_pos = lax.broadcasted_iota(jnp.int32, (block, 1), 0)
    dims_nt = (((1,), (1,)), ((), ()))
    dims_tn = (((0,), (0,)), ((), ()))

    for i in range(3):
        before = jnp.where(info[4 + i] > 0, info[i], 0)
        limit = jnp.where(in_own, info[i + 1], before)
        allowed = key_pos < limit
        row_weight = jnp.where(query_pos < info[i + 1], weight[i], 0.0)
        rows = slice(i * block, (i + 1) * block)
        span = slice(i * block, (i + 2) * block)
        for h in range(heads):
            cols = slice(h * head_size, (h + 1) * head_size)
            q = qn[h, rows, :]
            k = kn[h, span, :]
            v = vn[h, span, :]
            scores = lax.dot_general(q, k, dims_nt, preferred_element_type=f32) * scale
            expo = jnp.where(allowed, jnp.exp(scores), 0.0)
            probs = expo * (1.0 / jnp.sum(expo, axis=-1, keepdims=True))
            probs_cast = probs.astype(bf16)
            attended = jnp.dot(probs_cast, v, preferred_element_type=f32).astype(bf16)
            goal = tgt[rows, cols]
            if i == 2:
                goal = jnp.where(info[8] > 0, goal, jnp.zeros_like(goal))
            diff = attended.astype(f32) - goal.astype(f32)
            weighted = row_weight * diff
            if i < 2:
                squares = jnp.sum(weighted * diff, axis=0, keepdims=True)
                loss[0:1, :] += squares
            grad = (loss_scale * weighted).astype(bf16)
            prob_grad = lax.dot_general(grad, v, dims_nt, preferred_element_type=f32)
            delta = jnp.sum(probs * prob_grad, axis=-1, keepdims=True)
            score_grad = (probs * (prob_grad - delta) * scale).astype(bf16)
            if i < 2:
                dq[h, rows, :] = jnp.dot(score_grad, k, preferred_element_type=f32)
            if i < 2:
                own = slice(i * block, (i + 1) * block)
                dv[h, own, :] += lax.dot_general(
                    probs_cast[:, block:], grad, dims_tn, preferred_element_type=f32)
                dk[h, own, :] += lax.dot_general(
                    score_grad[:, block:], q, dims_tn, preferred_element_type=f32)
            if i > 0:
                own = slice((i - 1) * block, i * block)
                dv[h, own, :] += lax.dot_general(
                    probs_cast[:, :block], grad, dims_tn, preferred_element_type=f32)
                dk[h, own, :] += lax.dot_general(
                    score_grad[:, :block], q, dims_tn, preferred_element_type=f32)

    def norm_back(upstream, raw, gain):
        factor = lax.rsqrt(jnp.mean(raw * raw, axis=-1, keepdims=True) + epsilon)
        unit = raw * factor
        s = upstream * gain
        return (factor * (s - unit * jnp.mean(s * unit, axis=-1, keepdims=True))).astype(bf16)

    for h in range(heads):
        cols = slice(h * head_size, (h + 1) * head_size)
        back[0, :, cols] = norm_back(dq[h], raw_q[h], q_gain)
        back[1, :, cols] = norm_back(dk[h], raw_k[h], k_gain)
        back[2, :, cols] = dv[h].astype(bf16)

    depth = w.shape[1]
    step = 512
    for start in range(0, depth, step):
        total = lax.dot_general(
            back[0], w[0, start : start + step, :], dims_nt, preferred_element_type=f32)
        for j in (1, 2):
            total += lax.dot_general(
                back[j], w[j, start : start + step, :], dims_nt, preferred_element_type=f32)
        out[:, start : start + step] = total.astype(bf16)


def layer(info, weight, tok, tgt, w, q_gain, k_gain, block):
    head_size = q_gain.shape[0]
    depth, part = w.shape[1], w.shape[2]
    heads = part // head_size
    vmem = pl.BlockSpec(memory_space=pltpu.VMEM)
    smem = pl.BlockSpec(memory_space=pltpu.SMEM)
    f32, bf16 = jnp.float32, jnp.bfloat16
    return pl.pallas_call(
        functools.partial(layer_kernel, heads, head_size, block),
        out_shape=(
            jax.ShapeDtypeStruct((2 * block, depth), bf16),
            jax.ShapeDtypeStruct((8, 128), f32),
        ),
        in_specs=[smem, smem, vmem, vmem, vmem, vmem, vmem],
        out_specs=(vmem, vmem),
        scratch_shapes=[
            pltpu.VMEM((heads, 2 * block, head_size), f32),
            pltpu.VMEM((heads, 2 * block, head_size), f32),
            pltpu.VMEM((heads, 3 * block, head_size), bf16),
            pltpu.VMEM((heads, 4 * block, head_size), bf16),
            pltpu.VMEM((heads, 4 * block, head_size), bf16),
            pltpu.VMEM((heads, 2 * block, head_size), f32),
            pltpu.VMEM((heads, 2 * block, head_size), f32),
            pltpu.VMEM((heads, 2 * block, head_size), f32),
            pltpu.VMEM((3, 2 * block, part), bf16),
        ],
        compiler_params=pltpu.CompilerParams(vmem_limit_bytes=48 * 1024 * 1024),
    )(info, weight, tok, tgt, w, q_gain.reshape(1, head_size), k_gain.reshape(1, head_size))


def share_kernel(
    n, part, loss, out, loss_out, cbuf, ysend, yrecv, lbuf,
    c_send, c_recv, y_sem, l_send, l_recv,
):
    g, t = lax.axis_index("groups"), lax.axis_index("tm")
    k = t % QUAD
    y, c = k // 2, k % 2
    ynbr = (g, t + 2 - 4 * y)
    cnbr = (g, t + 1 - 2 * c)
    barrier = pltpu.get_barrier_semaphore()

    @pl.loop(1, n)
    def _(d):
        pl.semaphore_signal(
            barrier, inc=1, device_id=(g, (t + d) % n), device_id_type=MESH)

    pl.semaphore_wait(barrier, n - 1)

    def to_core(row):
        return pltpu.make_async_remote_copy(
            src_ref=part.at[2 * row + 1 - c], dst_ref=cbuf.at[row],
            send_sem=c_send.at[row], recv_sem=c_recv.at[row],
            device_id=cnbr, device_id_type=MESH,
        )

    to_core(1 - y).start()
    to_core(y).start()
    lbuf[t] = loss[...]

    def to_all(d):
        return pltpu.make_async_remote_copy(
            src_ref=loss, dst_ref=lbuf.at[t], send_sem=l_send.at[d],
            recv_sem=l_recv.at[t], device_id=(g, (t + d) % n), device_id_type=MESH,
        )

    def from_all(d):
        source = (t + d) % n
        return pltpu.make_async_remote_copy(
            src_ref=loss, dst_ref=lbuf.at[source], send_sem=l_send.at[d],
            recv_sem=l_recv.at[source], device_id=(g, source), device_id_type=MESH,
        )

    @pl.loop(1, n)
    def _(d):
        to_all(d).start()

    to_y = pltpu.make_async_remote_copy(
        src_ref=ysend, dst_ref=yrecv, send_sem=y_sem.at[0], recv_sem=y_sem.at[1],
        device_id=ynbr, device_id_type=MESH,
    )

    def arrived(row):
        return pltpu.make_async_remote_copy(
            src_ref=part.at[2 * row + 1 - c], dst_ref=cbuf.at[row],
            send_sem=c_send.at[row], recv_sem=c_recv.at[row],
            device_id=cnbr, device_id_type=MESH,
        )

    arrived(1 - y).wait_recv()
    ysend[...] = (
        part[2 * (1 - y) + c].astype(jnp.float32) + cbuf[1 - y].astype(jnp.float32)
    ).astype(jnp.bfloat16)
    to_y.start()
    arrived(y).wait_recv()

    @pl.loop(1, n)
    def _(d):
        from_all(d).wait_recv()

    total = jnp.sum(lbuf[...], axis=0)
    loss_out[...] = jnp.broadcast_to(jnp.sum(total), loss_out.shape)

    to_y.wait_recv()
    out[...] = (
        part[k].astype(jnp.float32) + cbuf[y].astype(jnp.float32) + yrecv[...].astype(jnp.float32)
    ).astype(jnp.bfloat16)
    to_y.wait_send()
    to_core(1 - y).wait_send()
    to_core(y).wait_send()

    @pl.loop(1, n)
    def _(d):
        to_all(d).wait_send()


def share(part, loss, n):
    _, rows, depth = part.shape
    dma = pltpu.SemaphoreType.DMA
    vmem = pl.BlockSpec(memory_space=pltpu.VMEM)
    bf16 = jnp.bfloat16
    return pl.pallas_call(
        functools.partial(share_kernel, n),
        out_shape=(
            jax.ShapeDtypeStruct((rows, depth), bf16),
            jax.ShapeDtypeStruct((8, 128), jnp.float32),
        ),
        in_specs=[vmem, vmem],
        out_specs=(vmem, vmem),
        scratch_shapes=[
            pltpu.VMEM((2, rows, depth), bf16),
            pltpu.VMEM((rows, depth), bf16),
            pltpu.VMEM((rows, depth), bf16),
            pltpu.VMEM((n, 8, 128), jnp.float32),
            dma((2,)), dma((2,)), dma((2,)), dma((n,)), dma((n,)),
        ],
        compiler_params=pltpu.CompilerParams(
            collective_id=1, has_side_effects=True, vmem_limit_bytes=24 * 1024 * 1024),
    )(part, loss)


def per_device(
    tokens, target, w_query, w_key, w_value, q_gain, k_gain, block_weight, block_reset, valid_count
):
    rows, width = tokens.shape
    n = lax.axis_size("tm")
    nz = n // QUAD
    block = 2 * rows
    z = lax.axis_index("tm") // QUAD
    blocks = valid_count.shape[0]
    index = 2 * z - 1 + jnp.arange(4, dtype=jnp.int32)
    inside = (index >= 0) & (index < blocks)
    hit = index[:, None] == jnp.arange(blocks, dtype=jnp.int32)[None, :]
    count = jnp.sum(jnp.where(hit, valid_count[None, :], 0), axis=1)
    reset = jnp.sum(jnp.where(hit, block_reset[None, :], 0), axis=1)
    weight = jnp.sum(jnp.where(hit, block_weight[None, :], 0.0), axis=1)[1:]
    count = jnp.where(inside | (index < 0), count, 1)
    sees = ((index[1:] > 0) & (reset[1:] == 0)).astype(jnp.int32)
    flags = jnp.stack([z > 0, z < nz - 1]).astype(jnp.int32)
    info = jnp.concatenate([count, sees, flags])

    tok, tgt, w = gather(tokens, target, w_query, w_key, w_value, n)
    part, loss = layer(
        info,
        weight,
        tok.reshape(8 * rows, width),
        tgt.reshape(6 * rows, -1),
        w.reshape(3, width, -1),
        q_gain,
        k_gain,
        block,
    )
    grad, loss_sum = share(part.reshape(QUAD, rows, width), loss, n)
    size = rows * n * w_query.shape[1]
    return grad, (loss_sum[0, :1] / size).reshape(1)


def solution(mesh):
    return jax.shard_map(
        per_device,
        mesh=mesh,
        in_specs=(
            P(("groups", "tm"), None),
            P(("groups", "tm"), None),
            P("tm", None),
            P("tm", None),
            P("tm", None),
            P(),
            P(),
            P("groups"),
            P("groups"),
            P("groups"),
        ),
        out_specs=(P(("groups", "tm"), None), P("groups")),
        check_vma=False,
    )
```

```python
import functools
import math

import jax
import jax.numpy as jnp
from jax import lax
from jax.experimental import pallas as pl
from jax.experimental.pallas import tpu as pltpu
from jax.sharding import PartitionSpec as P

epsilon = 1e-06
loss_scale = 32.0
QUAD = 4
MESH = pl.DeviceIdType.MESH
ORDER = (1, 2, 0)


def gather_kernel(
    nz, tok, tgt, wq, wk, wv, tokb, tgtb, wbuf,
    inj_recv, inj_send, inj_local,
    up_recv, up_send, dn_recv, dn_send, x_recv, x_send,
    tok_recv, tok_send, tok_local, tgt_recv, tgt_send, tgt_local,
):
    g, t = lax.axis_index("groups"), lax.axis_index("tm")
    z, k = t // QUAD, t % QUAD
    y, c = k // 2, k % 2
    part = wbuf.shape[3]
    weights = (wq, wk, wv)
    has_up, has_dn = z + 1 < nz, z > 0
    ynbr = (g, t + 2 - 4 * y)
    cnbr = (g, t + 1 - 2 * c)
    xnbr = (g + 1 - 2 * (g % 2), t)
    half = g % 2

    barrier = pltpu.get_barrier_semaphore()

    def greet(device):
        pl.semaphore_signal(barrier, inc=1, device_id=device, device_id_type=MESH)

    for d in range(1, QUAD):
        greet((g, QUAD * z + (k + d) % QUAD))
    greet(xnbr)

    @pl.when(has_up)
    def _():
        for m in range(QUAD):
            greet((g, QUAD * (z + 1) + m))

    @pl.when(has_dn)
    def _():
        for m in range(QUAD):
            greet((g, QUAD * (z - 1) + m))

    sides = jnp.where(has_up, 1, 0) + jnp.where(has_dn, 1, 0)
    pl.semaphore_wait(barrier, QUAD + QUAD * sides)

    def remote(src, dst, send_sem, recv_sem, device):
        return pltpu.make_async_remote_copy(
            src_ref=src, dst_ref=dst, send_sem=send_sem, recv_sem=recv_sem,
            device_id=device, device_id_type=MESH,
        )

    def columns(ref, m):
        return ref.at[:, pl.ds(pl.multiple_of(m * part, 128), part)]

    def inject(w, d):
        m = (k + d) % QUAD
        return remote(
            columns(weights[w], m), wbuf.at[w, t], inj_send.at[w, d - 1], inj_recv.at[w, k],
            (g, QUAD * z + m),
        )

    def injected(w, d):
        m = (k + d) % QUAD
        slot = wbuf.at[w, QUAD * z + m]
        return remote(slot, slot, inj_send.at[w, d - 1], inj_recv.at[w, m], (g, QUAD * z + m))

    def inject_own(w):
        return pltpu.make_async_copy(columns(weights[w], k), wbuf.at[w, t], inj_local.at[w])

    def piece(w, q, h):
        return wbuf.at[w, pl.ds(QUAD * q + 2 * h, 2)]

    def go_up(w, q):
        return remote(
            piece(w, q, half), piece(w, q, half), up_send.at[w, q], up_recv.at[w, q], (g, t + QUAD)
        )

    def go_dn(w, q):
        return remote(
            piece(w, q, half), piece(w, q, half), dn_send.at[w, q], dn_recv.at[w, q], (g, t - QUAD)
        )

    def go_x(w, q):
        return remote(
            piece(w, q, half), piece(w, q, half), x_send.at[w, q], x_recv.at[w, q], xnbr
        )

    def from_x(w, q):
        return remote(
            piece(w, q, 1 - half), piece(w, q, 1 - half), x_send.at[w, q], x_recv.at[w, q], xnbr
        )

    own_slot = 2 * (1 + y) + c
    their_slot = 2 * (2 - y) + c
    halo_slot = 6 * (1 - y) + c
    their_halo = 6 * y + c
    has_halo = jnp.where(y == 1, z, nz - 1 - z) > 0
    has_their_halo = jnp.where(y == 0, z, nz - 1 - z) > 0
    give_halo = jnp.where(y == 0, z, nz - 1 - z) > 0
    halo_to = (g, jnp.where(y == 0, t - QUAD, t + QUAD))
    halo_to_slot = 6 * (1 - y) + c

    def send_tok(src, slot, i, device):
        return remote(src, tokb.at[slot], tok_send.at[i], tok_recv.at[slot], device)

    own_y = send_tok(tok, own_slot, 0, ynbr)
    own_c = send_tok(tok, own_slot, 1, cnbr)
    own_z = send_tok(tok, halo_to_slot, 2, halo_to)
    halo_y = send_tok(tokb.at[halo_slot], halo_slot, 3, ynbr)
    halo_c = send_tok(tokb.at[halo_slot], halo_slot, 4, cnbr)
    their_c = send_tok(tokb.at[their_slot], their_slot, 5, cnbr)
    their_halo_c = send_tok(tokb.at[their_halo], their_halo, 6, cnbr)
    tok_own = pltpu.make_async_copy(tok, tokb.at[own_slot], tok_local.at[0])

    def tok_wait(slot):
        send_tok(tokb.at[slot], slot, 0, cnbr).wait_recv()

    def tgt_quad(d):
        m = (k + d) % QUAD
        return remote(
            columns(tgt, m), tgtb.at[k], tgt_send.at[d - 1], tgt_recv.at[k], (g, QUAD * z + m)
        )

    def tgt_before(m):
        return remote(
            columns(tgt, m), tgtb.at[QUAD + c], tgt_send.at[3 + m], tgt_recv.at[QUAD + c],
            (g, QUAD * (z - 1) + m),
        )

    tgt_own = pltpu.make_async_copy(columns(tgt, k), tgtb.at[k], tgt_local.at[0])

    def tgt_wait(slot):
        remote(
            tgtb.at[slot], tgtb.at[slot], tgt_send.at[0], tgt_recv.at[slot], cnbr
        ).wait_recv()

    gives_target = jnp.where(y == 0, z, 0) > 0

    for w in ORDER:
        for d in (2, 3, 1):
            inject(w, d).start()
        inject_own(w).start()
        if w == ORDER[0]:

            @pl.when(give_halo)
            def _():
                own_z.start()

    own_c.start()
    tok_own.start()
    tgt_own.start()

    for w in ORDER:
        for d in range(1, QUAD):
            injected(w, d).wait_recv()
        inject_own(w).wait()

        @pl.when(has_up)
        def _():
            go_up(w, z).start()

        @pl.when(has_dn)
        def _():
            go_dn(w, z).start()

    own_y.start()
    for d in range(1, QUAD):
        tgt_quad(d).start()

    @pl.when(gives_target)
    def _():
        for m in range(QUAD):
            tgt_before(m).start()

    def relay_halo():
        @pl.when(has_halo)
        def _():
            tok_wait(halo_slot)
            halo_y.start()
            halo_c.start()

    def relay_theirs():
        tok_wait(their_slot)
        their_c.start()

    def relay_their_halo():
        @pl.when(has_their_halo)
        def _():
            tok_wait(their_halo)
            their_halo_c.start()

    tasks = [relay_halo, relay_theirs, relay_their_halo]
    for s in range(1, nz):
        for w in ORDER:

            @pl.when(z - s >= 0)
            def _():
                go_up(w, z - s).wait_recv()

                @pl.when(has_up)
                def _():
                    go_up(w, z - s).start()

                go_x(w, z - s).start()

            @pl.when(z + s < nz)
            def _():
                go_dn(w, z + s).wait_recv()

                @pl.when(has_dn)
                def _():
                    go_dn(w, z + s).start()

                go_x(w, z + s).start()

        if tasks:
            tasks.pop(0)()
    for task in tasks:
        task()

    other = 1 - 2 * c
    tok_wait(2 + c + other)
    tok_wait(4 + c + other)

    @pl.when(has_dn)
    def _():
        tok_wait(c + other)

    @pl.when(has_up)
    def _():
        tok_wait(6 + c + other)

    for d in range(1, QUAD):
        tgt_wait((k + d) % QUAD)

    @pl.when(has_up)
    def _():
        tgt_wait(QUAD)
        tgt_wait(QUAD + 1)

    for s in range(1, nz):
        for w in ORDER:

            @pl.when(z - s >= 0)
            def _():
                from_x(w, z - s).wait_recv()

            @pl.when(z + s < nz)
            def _():
                from_x(w, z + s).wait_recv()

    tok_own.wait()
    tgt_own.wait()
    own_y.wait_send()
    own_c.wait_send()
    their_c.wait_send()

    @pl.when(give_halo)
    def _():
        own_z.wait_send()

    @pl.when(has_halo)
    def _():
        halo_y.wait_send()
        halo_c.wait_send()

    @pl.when(has_their_halo)
    def _():
        their_halo_c.wait_send()

    for d in range(1, QUAD):
        tgt_quad(d).wait_send()

    @pl.when(gives_target)
    def _():
        for m in range(QUAD):
            tgt_before(m).wait_send()

    for w in ORDER:
        for d in range(1, QUAD):
            inject(w, d).wait_send()

        @pl.when(has_up)
        def _():
            go_up(w, z).wait_send()

        @pl.when(has_dn)
        def _():
            go_dn(w, z).wait_send()

        for s in range(1, nz):

            @pl.when(z - s >= 0)
            def _():
                go_x(w, z - s).wait_send()

                @pl.when(has_up)
                def _():
                    go_up(w, z - s).wait_send()

            @pl.when(z + s < nz)
            def _():
                go_x(w, z + s).wait_send()

                @pl.when(has_dn)
                def _():
                    go_dn(w, z + s).wait_send()


def gather(tokens, target, w_query, w_key, w_value, n):
    nz = n // QUAD
    rows, width = tokens.shape
    depth = w_query.shape[0]
    part = w_query.shape[1] // QUAD
    dma = pltpu.SemaphoreType.DMA
    any_spec = pl.BlockSpec(memory_space=pl.ANY)
    return pl.pallas_call(
        functools.partial(gather_kernel, nz),
        out_shape=(
            jax.ShapeDtypeStruct((8, rows, width), jnp.bfloat16),
            jax.ShapeDtypeStruct((6, rows, part), jnp.bfloat16),
            jax.ShapeDtypeStruct((3, n, depth, part), jnp.bfloat16),
        ),
        in_specs=[any_spec] * 5,
        out_specs=(any_spec,) * 3,
        scratch_shapes=[
            dma((3, QUAD)), dma((3, QUAD - 1)), dma((3,)),
            dma((3, nz)), dma((3, nz)), dma((3, nz)), dma((3, nz)), dma((3, nz)), dma((3, nz)),
            dma((8,)), dma((7,)), dma((1,)), dma((6,)), dma((7,)), dma((1,)),
        ],
        compiler_params=pltpu.CompilerParams(collective_id=0, has_side_effects=True),
    )(tokens, target, w_query, w_key, w_value)


def layer_kernel(
    heads, head_size, block,
    valid_count, block_reset, block_weight, tok_hbm, tgt_hbm, w_hbm, qg, kg, back, loss,
    tok, tgt, w, raw_q, raw_k, qn, kn, vn, dq, dk, dv, sems,
):
    w_copies = [pltpu.make_async_copy(w_hbm.at[j], w.at[j], sems.at[j]) for j in range(3)]
    tok_copies = [
        pltpu.make_async_copy(
            tok_hbm.at[b * block : (b + 1) * block], tok.at[b * block : (b + 1) * block],
            sems.at[3 + b])
        for b in range(4)
    ]
    tgt_copy = pltpu.make_async_copy(tgt_hbm, tgt, sems.at[7])
    w_copies[1].start()
    tok_copies[0].start()
    w_copies[2].start()
    w_copies[0].start()
    for b in range(1, 4):
        tok_copies[b].start()
    tgt_copy.start()

    z = lax.axis_index("tm") // QUAD
    blocks = valid_count.shape[0]
    has_before = z > 0
    has_after = 2 * z + 2 < blocks
    places = [jnp.maximum(2 * z - 1, 0), 2 * z, 2 * z + 1, jnp.minimum(2 * z + 2, blocks - 1)]
    counts = [valid_count[p] for p in places]
    counts[0] = jnp.where(has_before, counts[0], 0)
    sees = [block_reset[p] == 0 for p in places[1:]]
    sees[0] = sees[0] & has_before
    weights = [block_weight[p] for p in places[1:]]
    weights[2] = jnp.where(has_after, weights[2], 0.0)

    scale = 1.0 / math.sqrt(head_size)
    q_gain, k_gain = qg[...], kg[...]
    f32, bf16 = jnp.float32, jnp.bfloat16

    def normed(raw, gain):
        factor = lax.rsqrt(jnp.mean(raw * raw, axis=-1, keepdims=True) + epsilon)
        return (raw * factor * gain).astype(bf16)

    for b in range(4):
        rows = slice(b * block, (b + 1) * block)
        tok_copies[b].wait()
        x = tok[rows, :]
        if b == 0:
            x = jnp.where(has_before, x, jnp.zeros_like(x))
            w_copies[1].wait()
        if b == 3:
            x = jnp.where(has_after, x, jnp.zeros_like(x))
        keys = jnp.dot(x, w[1], preferred_element_type=f32)
        if b == 0:
            w_copies[2].wait()
        values = jnp.dot(x, w[2], preferred_element_type=f32)
        if b == 1:
            w_copies[0].wait()
        if b > 0:
            queries = jnp.dot(x, w[0], preferred_element_type=f32)
        for h in range(heads):
            cols = slice(h * head_size, (h + 1) * head_size)
            kn[h, rows, :] = normed(keys[:, cols], k_gain)
            vn[h, rows, :] = values[:, cols].astype(bf16)
            if b > 0:
                qn[h, (b - 1) * block : b * block, :] = normed(queries[:, cols], q_gain)
            if b == 1 or b == 2:
                own = slice((b - 1) * block, b * block)
                raw_k[h, own, :] = keys[:, cols]
                raw_q[h, own, :] = queries[:, cols]

    tgt_copy.wait()
    dk[...] = jnp.zeros_like(dk)
    dv[...] = jnp.zeros_like(dv)
    loss[...] = jnp.zeros_like(loss)

    key_place = lax.broadcasted_iota(jnp.int32, (1, 2 * block), 1)
    in_own = key_place >= block
    key_pos = jnp.where(in_own, key_place - block, key_place)
    query_pos = lax.broadcasted_iota(jnp.int32, (block, 1), 0)
    dims_nt = (((1,), (1,)), ((), ()))
    dims_tn = (((0,), (0,)), ((), ()))

    for i in range(3):
        before = jnp.where(sees[i], counts[i], 0)
        limit = jnp.where(in_own, counts[i + 1], before)
        allowed = key_pos < limit
        row_weight = jnp.where(query_pos < counts[i + 1], weights[i], 0.0)
        rows = slice(i * block, (i + 1) * block)
        span = slice(i * block, (i + 2) * block)
        for h in range(heads):
            cols = slice(h * head_size, (h + 1) * head_size)
            q = qn[h, rows, :]
            k = kn[h, span, :]
            v = vn[h, span, :]
            scores = lax.dot_general(q, k, dims_nt, preferred_element_type=f32) * scale
            expo = jnp.where(allowed, jnp.exp(scores), 0.0)
            probs = expo * (1.0 / jnp.sum(expo, axis=-1, keepdims=True))
            probs_cast = probs.astype(bf16)
            attended = jnp.dot(probs_cast, v, preferred_element_type=f32).astype(bf16)
            goal = tgt[rows, cols]
            if i == 2:
                goal = jnp.where(has_after, goal, jnp.zeros_like(goal))
            diff = attended.astype(f32) - goal.astype(f32)
            weighted = row_weight * diff
            if i < 2:
                squares = jnp.sum(weighted * diff, axis=0, keepdims=True)
                loss[0:1, :] += squares
            grad = (loss_scale * weighted).astype(bf16)
            prob_grad = lax.dot_general(grad, v, dims_nt, preferred_element_type=f32)
            delta = jnp.sum(probs * prob_grad, axis=-1, keepdims=True)
            score_grad = (probs * (prob_grad - delta) * scale).astype(bf16)
            if i < 2:
                dq[h, rows, :] = jnp.dot(score_grad, k, preferred_element_type=f32)
            if i < 2:
                own = slice(i * block, (i + 1) * block)
                dv[h, own, :] += lax.dot_general(
                    probs_cast[:, block:], grad, dims_tn, preferred_element_type=f32)
                dk[h, own, :] += lax.dot_general(
                    score_grad[:, block:], q, dims_tn, preferred_element_type=f32)
            if i > 0:
                own = slice((i - 1) * block, i * block)
                dv[h, own, :] += lax.dot_general(
                    probs_cast[:, :block], grad, dims_tn, preferred_element_type=f32)
                dk[h, own, :] += lax.dot_general(
                    score_grad[:, :block], q, dims_tn, preferred_element_type=f32)

    def norm_back(upstream, raw, gain):
        factor = lax.rsqrt(jnp.mean(raw * raw, axis=-1, keepdims=True) + epsilon)
        unit = raw * factor
        s = upstream * gain
        return (factor * (s - unit * jnp.mean(s * unit, axis=-1, keepdims=True))).astype(bf16)

    for h in range(heads):
        cols = slice(h * head_size, (h + 1) * head_size)
        back[0, :, cols] = norm_back(dq[h], raw_q[h], q_gain)
        back[1, :, cols] = norm_back(dk[h], raw_k[h], k_gain)
        back[2, :, cols] = dv[h].astype(bf16)


def layer(valid_count, block_reset, block_weight, tok, tgt, w, q_gain, k_gain, block):
    head_size = q_gain.shape[0]
    depth, part = w.shape[1], w.shape[2]
    heads = part // head_size
    vmem = pl.BlockSpec(memory_space=pltpu.VMEM)
    smem = pl.BlockSpec(memory_space=pltpu.SMEM)
    any_spec = pl.BlockSpec(memory_space=pl.ANY)
    f32, bf16 = jnp.float32, jnp.bfloat16
    return pl.pallas_call(
        functools.partial(layer_kernel, heads, head_size, block),
        out_shape=(
            jax.ShapeDtypeStruct((3, 2 * block, part), bf16),
            jax.ShapeDtypeStruct((8, 128), f32),
        ),
        in_specs=[smem, smem, smem, any_spec, any_spec, any_spec, vmem, vmem],
        out_specs=(vmem, vmem),
        scratch_shapes=[
            pltpu.VMEM(tok.shape, bf16),
            pltpu.VMEM(tgt.shape, bf16),
            pltpu.VMEM(w.shape, bf16),
            pltpu.VMEM((heads, 2 * block, head_size), f32),
            pltpu.VMEM((heads, 2 * block, head_size), f32),
            pltpu.VMEM((heads, 3 * block, head_size), bf16),
            pltpu.VMEM((heads, 4 * block, head_size), bf16),
            pltpu.VMEM((heads, 4 * block, head_size), bf16),
            pltpu.VMEM((heads, 2 * block, head_size), f32),
            pltpu.VMEM((heads, 2 * block, head_size), f32),
            pltpu.VMEM((heads, 2 * block, head_size), f32),
            pltpu.SemaphoreType.DMA((8,)),
        ],
        compiler_params=pltpu.CompilerParams(vmem_limit_bytes=56 * 1024 * 1024),
    )(
        valid_count, block_reset, block_weight, tok, tgt, w,
        q_gain.reshape(1, head_size), k_gain.reshape(1, head_size),
    )


CHUNKS = 3


def share_kernel(
    n, back, w_hbm, loss, out, loss_out, w, part, cbuf, ysend, yrecv, lbuf,
    w_sem, c_send, c_recv, y_send, y_recv, l_send, l_recv,
):
    g, t = lax.axis_index("groups"), lax.axis_index("tm")
    k = t % QUAD
    y, c = k // 2, k % 2
    ynbr = (g, t + 2 - 4 * y)
    cnbr = (g, t + 1 - 2 * c)
    f32, bf16 = jnp.float32, jnp.bfloat16
    rows, depth = out.shape
    step = depth // CHUNKS

    def w_copy(i):
        span = slice(i * step, (i + 1) * step)
        return pltpu.make_async_copy(w_hbm.at[:, span], w.at[:, span], w_sem.at[i])

    for i in range(CHUNKS):
        w_copy(i).start()

    barrier = pltpu.get_barrier_semaphore()

    @pl.loop(1, n)
    def _(d):
        pl.semaphore_signal(
            barrier, inc=1, device_id=(g, (t + d) % n), device_id_type=MESH)

    def compute(i):
        span = slice(i * step, (i + 1) * step)
        w_copy(i).wait()
        total = None
        for j in range(3):
            term = lax.dot_general(
                back[j], w[j, span, :], (((1,), (1,)), ((), ())), preferred_element_type=f32)
            total = term if total is None else total + term
        for m in range(QUAD):
            part[i, m] = total[m * rows : (m + 1) * rows].astype(bf16)

    def to_core(i, row):
        return pltpu.make_async_remote_copy(
            src_ref=part.at[i, 2 * row + 1 - c], dst_ref=cbuf.at[i, row],
            send_sem=c_send.at[i, row], recv_sem=c_recv.at[i, row],
            device_id=cnbr, device_id_type=MESH,
        )

    def to_y(i):
        return pltpu.make_async_remote_copy(
            src_ref=ysend.at[i], dst_ref=yrecv.at[i], send_sem=y_send.at[i],
            recv_sem=y_recv.at[i], device_id=ynbr, device_id_type=MESH,
        )

    def pass_on(i):
        to_core(i, 1 - y).wait_recv()
        ysend[i] = (
            part[i, 2 * (1 - y) + c].astype(f32) + cbuf[i, 1 - y].astype(f32)
        ).astype(bf16)
        to_y(i).start()

    def to_all(d):
        return pltpu.make_async_remote_copy(
            src_ref=loss, dst_ref=lbuf.at[t], send_sem=l_send.at[d],
            recv_sem=l_recv.at[t], device_id=(g, (t + d) % n), device_id_type=MESH,
        )

    def from_all(d):
        source = (t + d) % n
        return pltpu.make_async_remote_copy(
            src_ref=loss, dst_ref=lbuf.at[source], send_sem=l_send.at[d],
            recv_sem=l_recv.at[source], device_id=(g, source), device_id_type=MESH,
        )

    compute(0)
    lbuf[t] = loss[...]
    pl.semaphore_wait(barrier, n - 1)
    to_core(0, 1 - y).start()
    to_core(0, y).start()

    for i in range(1, CHUNKS):
        compute(i)
        to_core(i, 1 - y).start()
        to_core(i, y).start()
        pass_on(i - 1)
    pass_on(CHUNKS - 1)

    @pl.loop(1, n)
    def _(d):
        to_all(d).start()

    @pl.loop(1, n)
    def _(d):
        from_all(d).wait_recv()

    total = jnp.sum(lbuf[...], axis=0)
    loss_out[...] = jnp.broadcast_to(jnp.sum(total), loss_out.shape)

    for i in range(CHUNKS):
        to_core(i, y).wait_recv()
        to_y(i).wait_recv()
        out[:, i * step : (i + 1) * step] = (
            part[i, k].astype(f32) + cbuf[i, y].astype(f32) + yrecv[i].astype(f32)
        ).astype(bf16)
    for i in range(CHUNKS):
        to_y(i).wait_send()
        to_core(i, 1 - y).wait_send()
        to_core(i, y).wait_send()

    @pl.loop(1, n)
    def _(d):
        to_all(d).wait_send()


def share(back, w, loss, n):
    rows = back.shape[1] // QUAD
    depth = w.shape[1]
    step = depth // CHUNKS
    dma = pltpu.SemaphoreType.DMA
    vmem = pl.BlockSpec(memory_space=pltpu.VMEM)
    bf16 = jnp.bfloat16
    return pl.pallas_call(
        functools.partial(share_kernel, n),
        out_shape=(
            jax.ShapeDtypeStruct((rows, depth), bf16),
            jax.ShapeDtypeStruct((8, 128), jnp.float32),
        ),
        in_specs=[vmem, pl.BlockSpec(memory_space=pl.ANY), vmem],
        out_specs=(vmem, vmem),
        scratch_shapes=[
            pltpu.VMEM(w.shape, bf16),
            pltpu.VMEM((CHUNKS, QUAD, rows, step), bf16),
            pltpu.VMEM((CHUNKS, 2, rows, step), bf16),
            pltpu.VMEM((CHUNKS, rows, step), bf16),
            pltpu.VMEM((CHUNKS, rows, step), bf16),
            pltpu.VMEM((n, 8, 128), jnp.float32),
            dma((CHUNKS,)), dma((CHUNKS, 2)), dma((CHUNKS, 2)), dma((CHUNKS,)), dma((CHUNKS,)),
            dma((n,)), dma((n,)),
        ],
        compiler_params=pltpu.CompilerParams(
            collective_id=1, has_side_effects=True, vmem_limit_bytes=48 * 1024 * 1024),
    )(back, w, loss)


def per_device(
    tokens, target, w_query, w_key, w_value, q_gain, k_gain, block_weight, block_reset, valid_count
):
    rows, width = tokens.shape
    n = lax.axis_size("tm")
    block = 2 * rows
    tok, tgt, w = gather(tokens, target, w_query, w_key, w_value, n)
    w = w.reshape(3, width, -1)
    back, loss = layer(
        valid_count,
        block_reset,
        block_weight,
        tok.reshape(8 * rows, width),
        tgt.reshape(6 * rows, -1),
        w,
        q_gain,
        k_gain,
        block,
    )
    grad, loss_sum = share(back, w, loss, n)
    size = rows * n * w_query.shape[1]
    return grad, (loss_sum[0, :1] / size).reshape(1)


def solution(mesh):
    return jax.shard_map(
        per_device,
        mesh=mesh,
        in_specs=(
            P(("groups", "tm"), None),
            P(("groups", "tm"), None),
            P("tm", None),
            P("tm", None),
            P("tm", None),
            P(),
            P(),
            P("groups"),
            P("groups"),
            P("groups"),
        ),
        out_specs=(P(("groups", "tm"), None), P("groups")),
        check_vma=False,
    )
```

```python
import functools
import math

import jax
import jax.numpy as jnp
from jax import lax
from jax.experimental import pallas as pl
from jax.experimental.pallas import tpu as pltpu
from jax.sharding import PartitionSpec as P

epsilon = 1e-06
loss_scale = 32.0
QUAD = 4
MESH = pl.DeviceIdType.MESH
ORDER = (1, 2, 0)


def gather_kernel(
    nz, tok, tgt, wq, wk, wv, tokb, tgtb, wbuf,
    inj_recv, inj_send, inj_local,
    up_recv, up_send, dn_recv, dn_send, x_recv, x_send,
    tok_recv, tok_send, tok_local, tgt_recv, tgt_send, tgt_local,
):
    g, t = lax.axis_index("groups"), lax.axis_index("tm")
    z, k = t // QUAD, t % QUAD
    y, c = k // 2, k % 2
    part = wbuf.shape[3]
    weights = (wq, wk, wv)
    has_up, has_dn = z + 1 < nz, z > 0
    ynbr = (g, t + 2 - 4 * y)
    cnbr = (g, t + 1 - 2 * c)
    xnbr = (g + 1 - 2 * (g % 2), t)
    half = g % 2

    barrier = pltpu.get_barrier_semaphore()

    def greet(device):
        pl.semaphore_signal(barrier, inc=1, device_id=device, device_id_type=MESH)

    for d in range(1, QUAD):
        greet((g, QUAD * z + (k + d) % QUAD))
    greet(xnbr)

    @pl.when(has_up)
    def _():
        for m in range(QUAD):
            greet((g, QUAD * (z + 1) + m))

    @pl.when(has_dn)
    def _():
        for m in range(QUAD):
            greet((g, QUAD * (z - 1) + m))

    sides = jnp.where(has_up, 1, 0) + jnp.where(has_dn, 1, 0)
    pl.semaphore_wait(barrier, QUAD + QUAD * sides)

    def remote(src, dst, send_sem, recv_sem, device):
        return pltpu.make_async_remote_copy(
            src_ref=src, dst_ref=dst, send_sem=send_sem, recv_sem=recv_sem,
            device_id=device, device_id_type=MESH,
        )

    def columns(ref, m):
        return ref.at[:, pl.ds(pl.multiple_of(m * part, 128), part)]

    def inject(w, d):
        m = (k + d) % QUAD
        return remote(
            columns(weights[w], m), wbuf.at[w, t], inj_send.at[w, d - 1], inj_recv.at[w, k],
            (g, QUAD * z + m),
        )

    def injected(w, d):
        m = (k + d) % QUAD
        slot = wbuf.at[w, QUAD * z + m]
        return remote(slot, slot, inj_send.at[w, d - 1], inj_recv.at[w, m], (g, QUAD * z + m))

    def inject_own(w):
        return pltpu.make_async_copy(columns(weights[w], k), wbuf.at[w, t], inj_local.at[w])

    def piece(w, q, h):
        return wbuf.at[w, pl.ds(QUAD * q + 2 * h, 2)]

    def go_up(w, q):
        return remote(
            piece(w, q, half), piece(w, q, half), up_send.at[w, q], up_recv.at[w, q], (g, t + QUAD)
        )

    def go_dn(w, q):
        return remote(
            piece(w, q, half), piece(w, q, half), dn_send.at[w, q], dn_recv.at[w, q], (g, t - QUAD)
        )

    def go_x(w, q):
        return remote(
            piece(w, q, half), piece(w, q, half), x_send.at[w, q], x_recv.at[w, q], xnbr
        )

    def from_x(w, q):
        return remote(
            piece(w, q, 1 - half), piece(w, q, 1 - half), x_send.at[w, q], x_recv.at[w, q], xnbr
        )

    own_slot = 2 * (1 + y) + c
    their_slot = 2 * (2 - y) + c
    upper = y == 1

    def send_tok(src, slot, i, device):
        return remote(src, tokb.at[slot], tok_send.at[i], tok_recv.at[slot], device)

    own_y = send_tok(tok, own_slot, 0, ynbr)
    own_c = send_tok(tok, own_slot, 1, cnbr)
    own_z = send_tok(tok, c, 2, (g, t + QUAD))
    their_c = send_tok(tokb.at[their_slot], their_slot, 3, cnbr)
    their_z = remote(
        tokb.at[their_slot], tokb.at[6 + c], tok_send.at[4], tok_recv.at[6 + c], (g, t - QUAD)
    )
    before_y = send_tok(tokb.at[c], c, 5, ynbr)
    before_c = send_tok(tokb.at[c], c, 6, cnbr)
    after_y = send_tok(tokb.at[6 + c], 6 + c, 7, ynbr)
    after_c = send_tok(tokb.at[6 + c], 6 + c, 8, cnbr)
    tok_own = pltpu.make_async_copy(tok, tokb.at[own_slot], tok_local.at[0])

    def tok_wait(slot):
        send_tok(tokb.at[slot], slot, 0, cnbr).wait_recv()

    def tgt_quad(d):
        m = (k + d) % QUAD
        return remote(
            columns(tgt, m), tgtb.at[k], tgt_send.at[d - 1], tgt_recv.at[k], (g, QUAD * z + m)
        )

    def tgt_before(m):
        return remote(
            columns(tgt, m), tgtb.at[QUAD + c], tgt_send.at[3 + m], tgt_recv.at[QUAD + c],
            (g, QUAD * (z - 1) + m),
        )

    tgt_own = pltpu.make_async_copy(columns(tgt, k), tgtb.at[k], tgt_local.at[0])

    def tgt_wait(slot):
        remote(
            tgtb.at[slot], tgtb.at[slot], tgt_send.at[0], tgt_recv.at[slot], cnbr
        ).wait_recv()

    gives_target = jnp.where(y == 0, z, 0) > 0

    for w in ORDER:
        for d in (2, 3, 1):
            inject(w, d).start()
        inject_own(w).start()
        if w == ORDER[0]:

            @pl.when(upper & has_up)
            def _():
                own_z.start()

    own_c.start()
    tok_own.start()
    tgt_own.start()

    for w in ORDER:
        for d in range(1, QUAD):
            injected(w, d).wait_recv()
        inject_own(w).wait()

        @pl.when(has_up)
        def _():
            go_up(w, z).start()

        @pl.when(has_dn)
        def _():
            go_dn(w, z).start()

    own_y.start()
    for d in range(1, QUAD):
        tgt_quad(d).start()

    @pl.when(gives_target)
    def _():
        for m in range(QUAD):
            tgt_before(m).start()

    def relay_theirs():
        tok_wait(their_slot)
        their_c.start()

        @pl.when(upper & has_dn)
        def _():
            their_z.start()

    def relay_before():
        @pl.when(has_dn)
        def _():
            tok_wait(c)
            before_c.start()

            @pl.when(upper)
            def _():
                before_y.start()

    def relay_after():
        @pl.when(has_up)
        def _():
            tok_wait(6 + c)
            after_c.start()

            @pl.when(upper)
            def _():
                after_y.start()

    def early():
        relay_theirs()

        @pl.when(upper)
        def _():
            relay_before()

    def middle():
        @pl.when(upper)
        def _():
            relay_after()

        @pl.when(jnp.logical_not(upper))
        def _():
            relay_before()

    def late():
        @pl.when(jnp.logical_not(upper))
        def _():
            relay_after()

    tasks = [early, middle, late]
    for s in range(1, nz):
        for w in ORDER:

            @pl.when(z - s >= 0)
            def _():
                go_up(w, z - s).wait_recv()

                @pl.when(has_up)
                def _():
                    go_up(w, z - s).start()

                go_x(w, z - s).start()

            @pl.when(z + s < nz)
            def _():
                go_dn(w, z + s).wait_recv()

                @pl.when(has_dn)
                def _():
                    go_dn(w, z + s).start()

                go_x(w, z + s).start()

        if tasks:
            tasks.pop(0)()
    for task in tasks:
        task()

    other = 1 - 2 * c
    tok_wait(2 + c + other)
    tok_wait(4 + c + other)

    @pl.when(has_dn)
    def _():
        tok_wait(c + other)

    @pl.when(has_up)
    def _():
        tok_wait(6 + c + other)

    for d in range(1, QUAD):
        tgt_wait((k + d) % QUAD)

    @pl.when(has_up)
    def _():
        tgt_wait(QUAD)
        tgt_wait(QUAD + 1)

    for s in range(1, nz):
        for w in ORDER:

            @pl.when(z - s >= 0)
            def _():
                from_x(w, z - s).wait_recv()

            @pl.when(z + s < nz)
            def _():
                from_x(w, z + s).wait_recv()

    tok_own.wait()
    tgt_own.wait()
    own_y.wait_send()
    own_c.wait_send()
    their_c.wait_send()

    @pl.when(upper & has_up)
    def _():
        own_z.wait_send()

    @pl.when(upper & has_dn)
    def _():
        their_z.wait_send()

    @pl.when(has_dn)
    def _():
        before_c.wait_send()

        @pl.when(upper)
        def _():
            before_y.wait_send()

    @pl.when(has_up)
    def _():
        after_c.wait_send()

        @pl.when(upper)
        def _():
            after_y.wait_send()

    for d in range(1, QUAD):
        tgt_quad(d).wait_send()

    @pl.when(gives_target)
    def _():
        for m in range(QUAD):
            tgt_before(m).wait_send()

    for w in ORDER:
        for d in range(1, QUAD):
            inject(w, d).wait_send()

        @pl.when(has_up)
        def _():
            go_up(w, z).wait_send()

        @pl.when(has_dn)
        def _():
            go_dn(w, z).wait_send()

        for s in range(1, nz):

            @pl.when(z - s >= 0)
            def _():
                go_x(w, z - s).wait_send()

                @pl.when(has_up)
                def _():
                    go_up(w, z - s).wait_send()

            @pl.when(z + s < nz)
            def _():
                go_x(w, z + s).wait_send()

                @pl.when(has_dn)
                def _():
                    go_dn(w, z + s).wait_send()


def gather(tokens, target, w_query, w_key, w_value, n):
    nz = n // QUAD
    rows, width = tokens.shape
    depth = w_query.shape[0]
    part = w_query.shape[1] // QUAD
    dma = pltpu.SemaphoreType.DMA
    any_spec = pl.BlockSpec(memory_space=pl.ANY)
    return pl.pallas_call(
        functools.partial(gather_kernel, nz),
        out_shape=(
            jax.ShapeDtypeStruct((8, rows, width), jnp.bfloat16),
            jax.ShapeDtypeStruct((6, rows, part), jnp.bfloat16),
            jax.ShapeDtypeStruct((3, n, depth, part), jnp.bfloat16),
        ),
        in_specs=[any_spec] * 5,
        out_specs=(any_spec,) * 3,
        scratch_shapes=[
            dma((3, QUAD)), dma((3, QUAD - 1)), dma((3,)),
            dma((3, nz)), dma((3, nz)), dma((3, nz)), dma((3, nz)), dma((3, nz)), dma((3, nz)),
            dma((8,)), dma((9,)), dma((1,)), dma((6,)), dma((7,)), dma((1,)),
        ],
        compiler_params=pltpu.CompilerParams(collective_id=0, has_side_effects=True),
    )(tokens, target, w_query, w_key, w_value)


def layer_kernel(
    heads, head_size, block,
    valid_count, block_reset, block_weight, tok_hbm, tgt_hbm, w_hbm, qg, kg, back, loss,
    tok, tgt, w, raw_q, raw_k, qn, kn, vn, dq, dk, dv, sems,
):
    w_copies = [pltpu.make_async_copy(w_hbm.at[j], w.at[j], sems.at[j]) for j in range(3)]
    tok_copies = [
        pltpu.make_async_copy(
            tok_hbm.at[b * block : (b + 1) * block], tok.at[b * block : (b + 1) * block],
            sems.at[3 + b])
        for b in range(4)
    ]
    tgt_copy = pltpu.make_async_copy(tgt_hbm, tgt, sems.at[7])
    w_copies[1].start()
    tok_copies[0].start()
    w_copies[2].start()
    w_copies[0].start()
    for b in range(1, 4):
        tok_copies[b].start()
    tgt_copy.start()

    z = lax.axis_index("tm") // QUAD
    blocks = valid_count.shape[0]
    has_before = z > 0
    has_after = 2 * z + 2 < blocks
    places = [jnp.maximum(2 * z - 1, 0), 2 * z, 2 * z + 1, jnp.minimum(2 * z + 2, blocks - 1)]
    counts = [valid_count[p] for p in places]
    counts[0] = jnp.where(has_before, counts[0], 0)
    sees = [block_reset[p] == 0 for p in places[1:]]
    sees[0] = sees[0] & has_before
    weights = [block_weight[p] for p in places[1:]]
    weights[2] = jnp.where(has_after, weights[2], 0.0)

    scale = 1.0 / math.sqrt(head_size)
    q_gain, k_gain = qg[...], kg[...]
    f32, bf16 = jnp.float32, jnp.bfloat16

    def normed(raw, gain):
        factor = lax.rsqrt(jnp.mean(raw * raw, axis=-1, keepdims=True) + epsilon)
        return (raw * factor * gain).astype(bf16)

    for b in range(4):
        rows = slice(b * block, (b + 1) * block)
        tok_copies[b].wait()
        x = tok[rows, :]
        if b == 0:
            x = jnp.where(has_before, x, jnp.zeros_like(x))
            w_copies[1].wait()
        if b == 3:
            x = jnp.where(has_after, x, jnp.zeros_like(x))
        keys = jnp.dot(x, w[1], preferred_element_type=f32)
        if b == 0:
            w_copies[2].wait()
        values = jnp.dot(x, w[2], preferred_element_type=f32)
        if b == 1:
            w_copies[0].wait()
        if b > 0:
            queries = jnp.dot(x, w[0], preferred_element_type=f32)
        for h in range(heads):
            cols = slice(h * head_size, (h + 1) * head_size)
            kn[h, rows, :] = normed(keys[:, cols], k_gain)
            vn[h, rows, :] = values[:, cols].astype(bf16)
            if b > 0:
                qn[h, (b - 1) * block : b * block, :] = normed(queries[:, cols], q_gain)
            if b == 1 or b == 2:
                own = slice((b - 1) * block, b * block)
                raw_k[h, own, :] = keys[:, cols]
                raw_q[h, own, :] = queries[:, cols]

    tgt_copy.wait()
    dk[...] = jnp.zeros_like(dk)
    dv[...] = jnp.zeros_like(dv)
    loss[...] = jnp.zeros_like(loss)

    key_place = lax.broadcasted_iota(jnp.int32, (1, 2 * block), 1)
    in_own = key_place >= block
    key_pos = jnp.where(in_own, key_place - block, key_place)
    query_pos = lax.broadcasted_iota(jnp.int32, (block, 1), 0)
    dims_nt = (((1,), (1,)), ((), ()))
    dims_tn = (((0,), (0,)), ((), ()))

    for i in range(3):
        before = jnp.where(sees[i], counts[i], 0)
        limit = jnp.where(in_own, counts[i + 1], before)
        allowed = key_pos < limit
        row_weight = jnp.where(query_pos < counts[i + 1], weights[i], 0.0)
        rows = slice(i * block, (i + 1) * block)
        span = slice(i * block, (i + 2) * block)
        for h in range(heads):
            cols = slice(h * head_size, (h + 1) * head_size)
            q = qn[h, rows, :]
            k = kn[h, span, :]
            v = vn[h, span, :]
            scores = lax.dot_general(q, k, dims_nt, preferred_element_type=f32) * scale
            expo = jnp.where(allowed, jnp.exp(scores), 0.0)
            probs = expo * (1.0 / jnp.sum(expo, axis=-1, keepdims=True))
            probs_cast = probs.astype(bf16)
            attended = jnp.dot(probs_cast, v, preferred_element_type=f32).astype(bf16)
            goal = tgt[rows, cols]
            if i == 2:
                goal = jnp.where(has_after, goal, jnp.zeros_like(goal))
            diff = attended.astype(f32) - goal.astype(f32)
            weighted = row_weight * diff
            if i < 2:
                squares = jnp.sum(weighted * diff, axis=0, keepdims=True)
                loss[0:1, :] += squares
            grad = (loss_scale * weighted).astype(bf16)
            prob_grad = lax.dot_general(grad, v, dims_nt, preferred_element_type=f32)
            delta = jnp.sum(probs * prob_grad, axis=-1, keepdims=True)
            score_grad = (probs * (prob_grad - delta) * scale).astype(bf16)
            if i < 2:
                dq[h, rows, :] = jnp.dot(score_grad, k, preferred_element_type=f32)
            if i < 2:
                own = slice(i * block, (i + 1) * block)
                dv[h, own, :] += lax.dot_general(
                    probs_cast[:, block:], grad, dims_tn, preferred_element_type=f32)
                dk[h, own, :] += lax.dot_general(
                    score_grad[:, block:], q, dims_tn, preferred_element_type=f32)
            if i > 0:
                own = slice((i - 1) * block, i * block)
                dv[h, own, :] += lax.dot_general(
                    probs_cast[:, :block], grad, dims_tn, preferred_element_type=f32)
                dk[h, own, :] += lax.dot_general(
                    score_grad[:, :block], q, dims_tn, preferred_element_type=f32)

    def norm_back(upstream, raw, gain):
        factor = lax.rsqrt(jnp.mean(raw * raw, axis=-1, keepdims=True) + epsilon)
        unit = raw * factor
        s = upstream * gain
        return (factor * (s - unit * jnp.mean(s * unit, axis=-1, keepdims=True))).astype(bf16)

    for h in range(heads):
        cols = slice(h * head_size, (h + 1) * head_size)
        back[0, :, cols] = norm_back(dq[h], raw_q[h], q_gain)
        back[1, :, cols] = norm_back(dk[h], raw_k[h], k_gain)
        back[2, :, cols] = dv[h].astype(bf16)


def layer(valid_count, block_reset, block_weight, tok, tgt, w, q_gain, k_gain, block):
    head_size = q_gain.shape[0]
    depth, part = w.shape[1], w.shape[2]
    heads = part // head_size
    vmem = pl.BlockSpec(memory_space=pltpu.VMEM)
    smem = pl.BlockSpec(memory_space=pltpu.SMEM)
    any_spec = pl.BlockSpec(memory_space=pl.ANY)
    f32, bf16 = jnp.float32, jnp.bfloat16
    return pl.pallas_call(
        functools.partial(layer_kernel, heads, head_size, block),
        out_shape=(
            jax.ShapeDtypeStruct((3, 2 * block, part), bf16),
            jax.ShapeDtypeStruct((8, 128), f32),
        ),
        in_specs=[smem, smem, smem, any_spec, any_spec, any_spec, vmem, vmem],
        out_specs=(vmem, vmem),
        scratch_shapes=[
            pltpu.VMEM(tok.shape, bf16),
            pltpu.VMEM(tgt.shape, bf16),
            pltpu.VMEM(w.shape, bf16),
            pltpu.VMEM((heads, 2 * block, head_size), f32),
            pltpu.VMEM((heads, 2 * block, head_size), f32),
            pltpu.VMEM((heads, 3 * block, head_size), bf16),
            pltpu.VMEM((heads, 4 * block, head_size), bf16),
            pltpu.VMEM((heads, 4 * block, head_size), bf16),
            pltpu.VMEM((heads, 2 * block, head_size), f32),
            pltpu.VMEM((heads, 2 * block, head_size), f32),
            pltpu.VMEM((heads, 2 * block, head_size), f32),
            pltpu.SemaphoreType.DMA((8,)),
        ],
        compiler_params=pltpu.CompilerParams(vmem_limit_bytes=58 * 1024 * 1024),
    )(
        valid_count, block_reset, block_weight, tok, tgt, w,
        q_gain.reshape(1, head_size), k_gain.reshape(1, head_size),
    )


CHUNKS = 3


def share_kernel(
    n, back_hbm, w_hbm, loss_hbm, out, loss_out, back, w, part, cbuf, ysend, yrecv, lbuf,
    w_sem, in_sem, c_send, c_recv, y_send, y_recv, l_send, l_recv,
):
    g, t = lax.axis_index("groups"), lax.axis_index("tm")
    k = t % QUAD
    y, c = k // 2, k % 2
    ynbr = (g, t + 2 - 4 * y)
    cnbr = (g, t + 1 - 2 * c)
    f32, bf16 = jnp.float32, jnp.bfloat16
    rows, depth = out.shape
    step = depth // CHUNKS

    def w_copy(i):
        span = slice(i * step, (i + 1) * step)
        return pltpu.make_async_copy(w_hbm.at[:, span], w.at[:, span], w_sem.at[i])

    back_copy = pltpu.make_async_copy(back_hbm, back, in_sem.at[0])
    loss_copy = pltpu.make_async_copy(loss_hbm, lbuf.at[t], in_sem.at[1])
    back_copy.start()
    for i in range(CHUNKS):
        w_copy(i).start()
    loss_copy.start()

    barrier = pltpu.get_barrier_semaphore()

    @pl.loop(1, n)
    def _(d):
        pl.semaphore_signal(
            barrier, inc=1, device_id=(g, (t + d) % n), device_id_type=MESH)

    def compute(i):
        span = slice(i * step, (i + 1) * step)
        w_copy(i).wait()
        total = None
        for j in range(3):
            term = lax.dot_general(
                back[j], w[j, span, :], (((1,), (1,)), ((), ())), preferred_element_type=f32)
            total = term if total is None else total + term
        for m in range(QUAD):
            part[i, m] = total[m * rows : (m + 1) * rows].astype(bf16)

    def to_core(i, row):
        return pltpu.make_async_remote_copy(
            src_ref=part.at[i, 2 * row + 1 - c], dst_ref=cbuf.at[i, row],
            send_sem=c_send.at[i, row], recv_sem=c_recv.at[i, row],
            device_id=cnbr, device_id_type=MESH,
        )

    def to_y(i):
        return pltpu.make_async_remote_copy(
            src_ref=ysend.at[i], dst_ref=yrecv.at[i], send_sem=y_send.at[i],
            recv_sem=y_recv.at[i], device_id=ynbr, device_id_type=MESH,
        )

    def pass_on(i):
        to_core(i, 1 - y).wait_recv()
        ysend[i] = (
            part[i, 2 * (1 - y) + c].astype(f32) + cbuf[i, 1 - y].astype(f32)
        ).astype(bf16)
        to_y(i).start()

    def to_all(d):
        return pltpu.make_async_remote_copy(
            src_ref=lbuf.at[t], dst_ref=lbuf.at[t], send_sem=l_send.at[d],
            recv_sem=l_recv.at[t], device_id=(g, (t + d) % n), device_id_type=MESH,
        )

    def from_all(d):
        source = (t + d) % n
        return pltpu.make_async_remote_copy(
            src_ref=lbuf.at[source], dst_ref=lbuf.at[source], send_sem=l_send.at[d],
            recv_sem=l_recv.at[source], device_id=(g, source), device_id_type=MESH,
        )

    back_copy.wait()
    compute(0)
    loss_copy.wait()
    pl.semaphore_wait(barrier, n - 1)
    to_core(0, 1 - y).start()
    to_core(0, y).start()

    for i in range(1, CHUNKS):
        compute(i)
        to_core(i, 1 - y).start()
        to_core(i, y).start()
        pass_on(i - 1)
    pass_on(CHUNKS - 1)

    @pl.loop(1, n)
    def _(d):
        to_all(d).start()

    @pl.loop(1, n)
    def _(d):
        from_all(d).wait_recv()

    total = jnp.sum(lbuf[...], axis=0)
    loss_out[...] = jnp.broadcast_to(jnp.sum(total), loss_out.shape)

    for i in range(CHUNKS):
        to_core(i, y).wait_recv()
        to_y(i).wait_recv()
        out[:, i * step : (i + 1) * step] = (
            part[i, k].astype(f32) + cbuf[i, y].astype(f32) + yrecv[i].astype(f32)
        ).astype(bf16)
    for i in range(CHUNKS):
        to_y(i).wait_send()
        to_core(i, 1 - y).wait_send()
        to_core(i, y).wait_send()

    @pl.loop(1, n)
    def _(d):
        to_all(d).wait_send()


def share(back, w, loss, n):
    rows = back.shape[1] // QUAD
    depth = w.shape[1]
    step = depth // CHUNKS
    dma = pltpu.SemaphoreType.DMA
    vmem = pl.BlockSpec(memory_space=pltpu.VMEM)
    bf16 = jnp.bfloat16
    return pl.pallas_call(
        functools.partial(share_kernel, n),
        out_shape=(
            jax.ShapeDtypeStruct((rows, depth), bf16),
            jax.ShapeDtypeStruct((8, 128), jnp.float32),
        ),
        in_specs=[pl.BlockSpec(memory_space=pl.ANY)] * 3,
        out_specs=(vmem, vmem),
        scratch_shapes=[
            pltpu.VMEM(back.shape, bf16),
            pltpu.VMEM(w.shape, bf16),
            pltpu.VMEM((CHUNKS, QUAD, rows, step), bf16),
            pltpu.VMEM((CHUNKS, 2, rows, step), bf16),
            pltpu.VMEM((CHUNKS, rows, step), bf16),
            pltpu.VMEM((CHUNKS, rows, step), bf16),
            pltpu.VMEM((n, 8, 128), jnp.float32),
            dma((CHUNKS,)), dma((2,)), dma((CHUNKS, 2)), dma((CHUNKS, 2)), dma((CHUNKS,)), dma((CHUNKS,)),
            dma((n,)), dma((n,)),
        ],
        compiler_params=pltpu.CompilerParams(
            collective_id=1, has_side_effects=True, vmem_limit_bytes=58 * 1024 * 1024),
    )(back, w, loss)


def per_device(
    tokens, target, w_query, w_key, w_value, q_gain, k_gain, block_weight, block_reset, valid_count
):
    rows, width = tokens.shape
    n = lax.axis_size("tm")
    block = 2 * rows
    tok, tgt, w = gather(tokens, target, w_query, w_key, w_value, n)
    w = w.reshape(3, width, -1)
    back, loss = layer(
        valid_count,
        block_reset,
        block_weight,
        tok.reshape(8 * rows, width),
        tgt.reshape(6 * rows, -1),
        w,
        q_gain,
        k_gain,
        block,
    )
    grad, loss_sum = share(back, w, loss, n)
    size = rows * n * w_query.shape[1]
    return grad, (loss_sum[0, :1] / size).reshape(1)


def solution(mesh):
    return jax.shard_map(
        per_device,
        mesh=mesh,
        in_specs=(
            P(("groups", "tm"), None),
            P(("groups", "tm"), None),
            P("tm", None),
            P("tm", None),
            P("tm", None),
            P(),
            P(),
            P("groups"),
            P("groups"),
            P("groups"),
        ),
        out_specs=(P(("groups", "tm"), None), P("groups")),
        check_vma=False,
    )
```

```python
import functools
import math

import jax
import jax.numpy as jnp
from jax import lax
from jax.experimental import pallas as pl
from jax.experimental.pallas import tpu as pltpu
from jax.sharding import PartitionSpec as P

epsilon = 1e-06
loss_scale = 32.0
QUAD = 4
MESH = pl.DeviceIdType.MESH
ORDER = (1, 2, 0)


def gather_kernel(
    nz, tok, tgt, wq, wk, wv, tokb, tgtb, wbuf,
    inj_recv, inj_send, inj_local,
    up_recv, up_send, dn_recv, dn_send, x_recv, x_send,
    tok_recv, tok_send, tok_local, tgt_recv, tgt_send, tgt_local,
):
    g, t = lax.axis_index("groups"), lax.axis_index("tm")
    z, k = t // QUAD, t % QUAD
    y, c = k // 2, k % 2
    part = wbuf.shape[3]
    weights = (wq, wk, wv)
    has_up, has_dn = z + 1 < nz, z > 0
    ynbr = (g, t + 2 - 4 * y)
    cnbr = (g, t + 1 - 2 * c)
    xnbr = (g + 1 - 2 * (g % 2), t)
    half = g % 2

    barrier = pltpu.get_barrier_semaphore()

    def greet(device):
        pl.semaphore_signal(barrier, inc=1, device_id=device, device_id_type=MESH)

    for d in range(1, QUAD):
        greet((g, QUAD * z + (k + d) % QUAD))
    greet(xnbr)

    @pl.when(has_up)
    def _():
        for m in range(QUAD):
            greet((g, QUAD * (z + 1) + m))

    @pl.when(has_dn)
    def _():
        for m in range(QUAD):
            greet((g, QUAD * (z - 1) + m))

    sides = jnp.where(has_up, 1, 0) + jnp.where(has_dn, 1, 0)
    pl.semaphore_wait(barrier, QUAD + QUAD * sides)

    def remote(src, dst, send_sem, recv_sem, device):
        return pltpu.make_async_remote_copy(
            src_ref=src, dst_ref=dst, send_sem=send_sem, recv_sem=recv_sem,
            device_id=device, device_id_type=MESH,
        )

    def columns(ref, m):
        return ref.at[:, pl.ds(pl.multiple_of(m * part, 128), part)]

    def inject(w, d):
        m = (k + d) % QUAD
        return remote(
            columns(weights[w], m), wbuf.at[w, t], inj_send.at[w, d - 1], inj_recv.at[w, k],
            (g, QUAD * z + m),
        )

    def injected(w, d):
        m = (k + d) % QUAD
        slot = wbuf.at[w, QUAD * z + m]
        return remote(slot, slot, inj_send.at[w, d - 1], inj_recv.at[w, m], (g, QUAD * z + m))

    def inject_own(w):
        return pltpu.make_async_copy(columns(weights[w], k), wbuf.at[w, t], inj_local.at[w])

    def piece(w, q, h):
        return wbuf.at[w, pl.ds(QUAD * q + 2 * h, 2)]

    def go_up(w, q):
        return remote(
            piece(w, q, half), piece(w, q, half), up_send.at[w, q], up_recv.at[w, q], (g, t + QUAD)
        )

    def go_dn(w, q):
        return remote(
            piece(w, q, half), piece(w, q, half), dn_send.at[w, q], dn_recv.at[w, q], (g, t - QUAD)
        )

    def go_x(w, q):
        return remote(
            piece(w, q, half), piece(w, q, half), x_send.at[w, q], x_recv.at[w, q], xnbr
        )

    def from_x(w, q):
        return remote(
            piece(w, q, 1 - half), piece(w, q, 1 - half), x_send.at[w, q], x_recv.at[w, q], xnbr
        )

    own_slot = 2 * (1 + y) + c
    their_slot = 2 * (2 - y) + c
    upper = y == 1

    def send_tok(src, slot, i, device):
        return remote(src, tokb.at[slot], tok_send.at[i], tok_recv.at[slot], device)

    own_y = send_tok(tok, own_slot, 0, ynbr)
    own_c = send_tok(tok, own_slot, 1, cnbr)
    own_z = send_tok(tok, c, 2, (g, t + QUAD))
    their_c = send_tok(tokb.at[their_slot], their_slot, 3, cnbr)
    their_z = remote(
        tokb.at[their_slot], tokb.at[6 + c], tok_send.at[4], tok_recv.at[6 + c], (g, t - QUAD)
    )
    before_y = send_tok(tokb.at[c], c, 5, ynbr)
    before_c = send_tok(tokb.at[c], c, 6, cnbr)
    after_y = send_tok(tokb.at[6 + c], 6 + c, 7, ynbr)
    after_c = send_tok(tokb.at[6 + c], 6 + c, 8, cnbr)
    tok_own = pltpu.make_async_copy(tok, tokb.at[own_slot], tok_local.at[0])

    def tok_wait(slot):
        send_tok(tokb.at[slot], slot, 0, cnbr).wait_recv()

    def tgt_quad(d):
        m = (k + d) % QUAD
        return remote(
            columns(tgt, m), tgtb.at[k], tgt_send.at[d - 1], tgt_recv.at[k], (g, QUAD * z + m)
        )

    def tgt_before(m):
        return remote(
            columns(tgt, m), tgtb.at[QUAD + c], tgt_send.at[3 + m], tgt_recv.at[QUAD + c],
            (g, QUAD * (z - 1) + m),
        )

    tgt_own = pltpu.make_async_copy(columns(tgt, k), tgtb.at[k], tgt_local.at[0])

    def tgt_wait(slot):
        remote(
            tgtb.at[slot], tgtb.at[slot], tgt_send.at[0], tgt_recv.at[slot], cnbr
        ).wait_recv()

    gives_target = jnp.where(y == 0, z, 0) > 0

    for w in ORDER:
        for d in (2, 3, 1):
            inject(w, d).start()
        inject_own(w).start()
        if w == ORDER[0]:

            @pl.when(upper & has_up)
            def _():
                own_z.start()

        for d in range(1, QUAD):
            injected(w, d).wait_recv()
        inject_own(w).wait()

        @pl.when(has_up)
        def _():
            go_up(w, z).start()

        @pl.when(has_dn)
        def _():
            go_dn(w, z).start()

    own_c.start()
    tok_own.start()
    tgt_own.start()
    own_y.start()
    for d in range(1, QUAD):
        tgt_quad(d).start()

    @pl.when(gives_target)
    def _():
        for m in range(QUAD):
            tgt_before(m).start()

    def relay_theirs():
        tok_wait(their_slot)
        their_c.start()

        @pl.when(upper & has_dn)
        def _():
            their_z.start()

    def relay_before():
        @pl.when(has_dn)
        def _():
            tok_wait(c)
            before_c.start()

            @pl.when(upper)
            def _():
                before_y.start()

    def relay_after():
        @pl.when(has_up)
        def _():
            tok_wait(6 + c)
            after_c.start()

            @pl.when(upper)
            def _():
                after_y.start()

    def early():
        relay_theirs()

        @pl.when(upper)
        def _():
            relay_before()

    def middle():
        @pl.when(upper)
        def _():
            relay_after()

        @pl.when(jnp.logical_not(upper))
        def _():
            relay_before()

    def late():
        @pl.when(jnp.logical_not(upper))
        def _():
            relay_after()

    tasks = [early, middle, late]
    for s in range(1, nz):
        for w in ORDER:

            @pl.when(z - s >= 0)
            def _():
                go_up(w, z - s).wait_recv()

                @pl.when(has_up)
                def _():
                    go_up(w, z - s).start()

                go_x(w, z - s).start()

            @pl.when(z + s < nz)
            def _():
                go_dn(w, z + s).wait_recv()

                @pl.when(has_dn)
                def _():
                    go_dn(w, z + s).start()

                go_x(w, z + s).start()

        if tasks:
            tasks.pop(0)()
    for task in tasks:
        task()

    other = 1 - 2 * c
    tok_wait(2 + c + other)
    tok_wait(4 + c + other)

    @pl.when(has_dn)
    def _():
        tok_wait(c + other)

    @pl.when(has_up)
    def _():
        tok_wait(6 + c + other)

    for d in range(1, QUAD):
        tgt_wait((k + d) % QUAD)

    @pl.when(has_up)
    def _():
        tgt_wait(QUAD)
        tgt_wait(QUAD + 1)

    for s in range(1, nz):
        for w in ORDER:

            @pl.when(z - s >= 0)
            def _():
                from_x(w, z - s).wait_recv()

            @pl.when(z + s < nz)
            def _():
                from_x(w, z + s).wait_recv()

    tok_own.wait()
    tgt_own.wait()
    own_y.wait_send()
    own_c.wait_send()
    their_c.wait_send()

    @pl.when(upper & has_up)
    def _():
        own_z.wait_send()

    @pl.when(upper & has_dn)
    def _():
        their_z.wait_send()

    @pl.when(has_dn)
    def _():
        before_c.wait_send()

        @pl.when(upper)
        def _():
            before_y.wait_send()

    @pl.when(has_up)
    def _():
        after_c.wait_send()

        @pl.when(upper)
        def _():
            after_y.wait_send()

    for d in range(1, QUAD):
        tgt_quad(d).wait_send()

    @pl.when(gives_target)
    def _():
        for m in range(QUAD):
            tgt_before(m).wait_send()

    for w in ORDER:
        for d in range(1, QUAD):
            inject(w, d).wait_send()

        @pl.when(has_up)
        def _():
            go_up(w, z).wait_send()

        @pl.when(has_dn)
        def _():
            go_dn(w, z).wait_send()

        for s in range(1, nz):

            @pl.when(z - s >= 0)
            def _():
                go_x(w, z - s).wait_send()

                @pl.when(has_up)
                def _():
                    go_up(w, z - s).wait_send()

            @pl.when(z + s < nz)
            def _():
                go_x(w, z + s).wait_send()

                @pl.when(has_dn)
                def _():
                    go_dn(w, z + s).wait_send()


def gather(tokens, target, w_query, w_key, w_value, n):
    nz = n // QUAD
    rows, width = tokens.shape
    depth = w_query.shape[0]
    part = w_query.shape[1] // QUAD
    dma = pltpu.SemaphoreType.DMA
    any_spec = pl.BlockSpec(memory_space=pl.ANY)
    return pl.pallas_call(
        functools.partial(gather_kernel, nz),
        out_shape=(
            jax.ShapeDtypeStruct((8, rows, width), jnp.bfloat16),
            jax.ShapeDtypeStruct((6, rows, part), jnp.bfloat16),
            jax.ShapeDtypeStruct((3, n, depth, part), jnp.bfloat16),
        ),
        in_specs=[any_spec] * 5,
        out_specs=(any_spec,) * 3,
        scratch_shapes=[
            dma((3, QUAD)), dma((3, QUAD - 1)), dma((3,)),
            dma((3, nz)), dma((3, nz)), dma((3, nz)), dma((3, nz)), dma((3, nz)), dma((3, nz)),
            dma((8,)), dma((9,)), dma((1,)), dma((6,)), dma((7,)), dma((1,)),
        ],
        compiler_params=pltpu.CompilerParams(collective_id=0, has_side_effects=True),
    )(tokens, target, w_query, w_key, w_value)


def layer_kernel(
    heads, head_size, block,
    valid_count, block_reset, block_weight, tok_hbm, tgt_hbm, w_hbm, qg, kg, back, loss,
    tok, tgt, w, raw_q, raw_k, qn, kn, vn, dq, dk, dv, sems,
):
    w_copies = [pltpu.make_async_copy(w_hbm.at[j], w.at[j], sems.at[j]) for j in range(3)]
    tok_copies = [
        pltpu.make_async_copy(
            tok_hbm.at[b * block : (b + 1) * block], tok.at[b * block : (b + 1) * block],
            sems.at[3 + b])
        for b in range(4)
    ]
    tgt_copy = pltpu.make_async_copy(tgt_hbm, tgt, sems.at[7])
    w_copies[1].start()
    tok_copies[0].start()
    w_copies[2].start()
    w_copies[0].start()
    for b in range(1, 4):
        tok_copies[b].start()
    tgt_copy.start()

    z = lax.axis_index("tm") // QUAD
    blocks = valid_count.shape[0]
    has_before = z > 0
    has_after = 2 * z + 2 < blocks
    places = [jnp.maximum(2 * z - 1, 0), 2 * z, 2 * z + 1, jnp.minimum(2 * z + 2, blocks - 1)]
    counts = [valid_count[p] for p in places]
    counts[0] = jnp.where(has_before, counts[0], 0)
    sees = [block_reset[p] == 0 for p in places[1:]]
    sees[0] = sees[0] & has_before
    weights = [block_weight[p] for p in places[1:]]
    weights[2] = jnp.where(has_after, weights[2], 0.0)

    scale = 1.0 / math.sqrt(head_size)
    q_gain, k_gain = qg[...], kg[...]
    f32, bf16 = jnp.float32, jnp.bfloat16

    def normed(raw, gain):
        factor = lax.rsqrt(jnp.mean(raw * raw, axis=-1, keepdims=True) + epsilon)
        return (raw * factor * gain).astype(bf16)

    for b in range(4):
        rows = slice(b * block, (b + 1) * block)
        tok_copies[b].wait()
        x = tok[rows, :]
        if b == 0:
            x = jnp.where(has_before, x, jnp.zeros_like(x))
            w_copies[1].wait()
        if b == 3:
            x = jnp.where(has_after, x, jnp.zeros_like(x))
        keys = jnp.dot(x, w[1], preferred_element_type=f32)
        if b == 0:
            w_copies[2].wait()
        values = jnp.dot(x, w[2], preferred_element_type=f32)
        if b == 1:
            w_copies[0].wait()
        if b > 0:
            queries = jnp.dot(x, w[0], preferred_element_type=f32)
        for h in range(heads):
            cols = slice(h * head_size, (h + 1) * head_size)
            kn[h, rows, :] = normed(keys[:, cols], k_gain)
            vn[h, rows, :] = values[:, cols].astype(bf16)
            if b > 0:
                qn[h, (b - 1) * block : b * block, :] = normed(queries[:, cols], q_gain)
            if b == 1 or b == 2:
                own = slice((b - 1) * block, b * block)
                raw_k[h, own, :] = keys[:, cols]
                raw_q[h, own, :] = queries[:, cols]

    tgt_copy.wait()
    dk[...] = jnp.zeros_like(dk)
    dv[...] = jnp.zeros_like(dv)
    loss[...] = jnp.zeros_like(loss)

    key_place = lax.broadcasted_iota(jnp.int32, (1, 2 * block), 1)
    in_own = key_place >= block
    key_pos = jnp.where(in_own, key_place - block, key_place)
    query_pos = lax.broadcasted_iota(jnp.int32, (block, 1), 0)
    dims_nt = (((1,), (1,)), ((), ()))
    dims_tn = (((0,), (0,)), ((), ()))

    for i in range(3):
        before = jnp.where(sees[i], counts[i], 0)
        limit = jnp.where(in_own, counts[i + 1], before)
        allowed = key_pos < limit
        row_weight = jnp.where(query_pos < counts[i + 1], weights[i], 0.0)
        rows = slice(i * block, (i + 1) * block)
        span = slice(i * block, (i + 2) * block)
        for h in range(heads):
            cols = slice(h * head_size, (h + 1) * head_size)
            q = qn[h, rows, :]
            k = kn[h, span, :]
            v = vn[h, span, :]
            scores = lax.dot_general(q, k, dims_nt, preferred_element_type=f32) * scale
            expo = jnp.where(allowed, jnp.exp(scores), 0.0)
            probs = expo * (1.0 / jnp.sum(expo, axis=-1, keepdims=True))
            probs_cast = probs.astype(bf16)
            attended = jnp.dot(probs_cast, v, preferred_element_type=f32).astype(bf16)
            goal = tgt[rows, cols]
            if i == 2:
                goal = jnp.where(has_after, goal, jnp.zeros_like(goal))
            diff = attended.astype(f32) - goal.astype(f32)
            weighted = row_weight * diff
            if i < 2:
                squares = jnp.sum(weighted * diff, axis=0, keepdims=True)
                loss[0:1, :] += squares
            grad = (loss_scale * weighted).astype(bf16)
            prob_grad = lax.dot_general(grad, v, dims_nt, preferred_element_type=f32)
            delta = jnp.sum(probs * prob_grad, axis=-1, keepdims=True)
            score_grad = (probs * (prob_grad - delta) * scale).astype(bf16)
            if i < 2:
                dq[h, rows, :] = jnp.dot(score_grad, k, preferred_element_type=f32)
            if i < 2:
                own = slice(i * block, (i + 1) * block)
                dv[h, own, :] += lax.dot_general(
                    probs_cast[:, block:], grad, dims_tn, preferred_element_type=f32)
                dk[h, own, :] += lax.dot_general(
                    score_grad[:, block:], q, dims_tn, preferred_element_type=f32)
            if i > 0:
                own = slice((i - 1) * block, i * block)
                dv[h, own, :] += lax.dot_general(
                    probs_cast[:, :block], grad, dims_tn, preferred_element_type=f32)
                dk[h, own, :] += lax.dot_general(
                    score_grad[:, :block], q, dims_tn, preferred_element_type=f32)

    def norm_back(upstream, raw, gain):
        factor = lax.rsqrt(jnp.mean(raw * raw, axis=-1, keepdims=True) + epsilon)
        unit = raw * factor
        s = upstream * gain
        return (factor * (s - unit * jnp.mean(s * unit, axis=-1, keepdims=True))).astype(bf16)

    for h in range(heads):
        cols = slice(h * head_size, (h + 1) * head_size)
        back[0, :, cols] = norm_back(dq[h], raw_q[h], q_gain)
        back[1, :, cols] = norm_back(dk[h], raw_k[h], k_gain)
        back[2, :, cols] = dv[h].astype(bf16)


def layer(valid_count, block_reset, block_weight, tok, tgt, w, q_gain, k_gain, block):
    head_size = q_gain.shape[0]
    depth, part = w.shape[1], w.shape[2]
    heads = part // head_size
    vmem = pl.BlockSpec(memory_space=pltpu.VMEM)
    smem = pl.BlockSpec(memory_space=pltpu.SMEM)
    any_spec = pl.BlockSpec(memory_space=pl.ANY)
    f32, bf16 = jnp.float32, jnp.bfloat16
    return pl.pallas_call(
        functools.partial(layer_kernel, heads, head_size, block),
        out_shape=(
            jax.ShapeDtypeStruct((3, 2 * block, part), bf16),
            jax.ShapeDtypeStruct((8, 128), f32),
        ),
        in_specs=[smem, smem, smem, any_spec, any_spec, any_spec, vmem, vmem],
        out_specs=(vmem, vmem),
        scratch_shapes=[
            pltpu.VMEM(tok.shape, bf16),
            pltpu.VMEM(tgt.shape, bf16),
            pltpu.VMEM(w.shape, bf16),
            pltpu.VMEM((heads, 2 * block, head_size), f32),
            pltpu.VMEM((heads, 2 * block, head_size), f32),
            pltpu.VMEM((heads, 3 * block, head_size), bf16),
            pltpu.VMEM((heads, 4 * block, head_size), bf16),
            pltpu.VMEM((heads, 4 * block, head_size), bf16),
            pltpu.VMEM((heads, 2 * block, head_size), f32),
            pltpu.VMEM((heads, 2 * block, head_size), f32),
            pltpu.VMEM((heads, 2 * block, head_size), f32),
            pltpu.SemaphoreType.DMA((8,)),
        ],
        compiler_params=pltpu.CompilerParams(vmem_limit_bytes=58 * 1024 * 1024),
    )(
        valid_count, block_reset, block_weight, tok, tgt, w,
        q_gain.reshape(1, head_size), k_gain.reshape(1, head_size),
    )


CHUNKS = 3


def share_kernel(
    n, back_hbm, w_hbm, loss_hbm, out, loss_out, back, w, part, cbuf, ysend, yrecv, lbuf,
    w_sem, in_sem, c_send, c_recv, y_send, y_recv, l_send, l_recv,
):
    g, t = lax.axis_index("groups"), lax.axis_index("tm")
    k = t % QUAD
    y, c = k // 2, k % 2
    ynbr = (g, t + 2 - 4 * y)
    cnbr = (g, t + 1 - 2 * c)
    f32, bf16 = jnp.float32, jnp.bfloat16
    rows, depth = out.shape
    step = depth // CHUNKS

    def w_copy(i):
        span = slice(i * step, (i + 1) * step)
        return pltpu.make_async_copy(w_hbm.at[:, span], w.at[:, span], w_sem.at[i])

    back_copy = pltpu.make_async_copy(back_hbm, back, in_sem.at[0])
    loss_copy = pltpu.make_async_copy(loss_hbm, lbuf.at[t], in_sem.at[1])
    back_copy.start()
    for i in range(CHUNKS):
        w_copy(i).start()
    loss_copy.start()

    barrier = pltpu.get_barrier_semaphore()

    @pl.loop(1, n)
    def _(d):
        pl.semaphore_signal(
            barrier, inc=1, device_id=(g, (t + d) % n), device_id_type=MESH)

    def compute(i):
        span = slice(i * step, (i + 1) * step)
        w_copy(i).wait()
        total = None
        for j in range(3):
            term = lax.dot_general(
                back[j], w[j, span, :], (((1,), (1,)), ((), ())), preferred_element_type=f32)
            total = term if total is None else total + term
        for m in range(QUAD):
            part[i, m] = total[m * rows : (m + 1) * rows].astype(bf16)

    def to_core(i, row):
        return pltpu.make_async_remote_copy(
            src_ref=part.at[i, 2 * row + 1 - c], dst_ref=cbuf.at[i, row],
            send_sem=c_send.at[i, row], recv_sem=c_recv.at[i, row],
            device_id=cnbr, device_id_type=MESH,
        )

    def to_y(i):
        return pltpu.make_async_remote_copy(
            src_ref=ysend.at[i], dst_ref=yrecv.at[i], send_sem=y_send.at[i],
            recv_sem=y_recv.at[i], device_id=ynbr, device_id_type=MESH,
        )

    def pass_on(i):
        to_core(i, 1 - y).wait_recv()
        ysend[i] = (
            part[i, 2 * (1 - y) + c].astype(f32) + cbuf[i, 1 - y].astype(f32)
        ).astype(bf16)
        to_y(i).start()

    def to_all(d):
        return pltpu.make_async_remote_copy(
            src_ref=lbuf.at[t], dst_ref=lbuf.at[t], send_sem=l_send.at[d],
            recv_sem=l_recv.at[t], device_id=(g, (t + d) % n), device_id_type=MESH,
        )

    def from_all(d):
        source = (t + d) % n
        return pltpu.make_async_remote_copy(
            src_ref=lbuf.at[source], dst_ref=lbuf.at[source], send_sem=l_send.at[d],
            recv_sem=l_recv.at[source], device_id=(g, source), device_id_type=MESH,
        )

    back_copy.wait()
    compute(0)
    loss_copy.wait()
    pl.semaphore_wait(barrier, n - 1)
    to_core(0, 1 - y).start()
    to_core(0, y).start()

    @pl.loop(1, n)
    def _(d):
        to_all(d).start()

    for i in range(1, CHUNKS):
        compute(i)
        to_core(i, 1 - y).start()
        to_core(i, y).start()
        pass_on(i - 1)
    pass_on(CHUNKS - 1)

    @pl.loop(1, n)
    def _(d):
        from_all(d).wait_recv()

    total = jnp.sum(lbuf[...], axis=0)
    loss_out[...] = jnp.broadcast_to(jnp.sum(total), loss_out.shape)

    for i in range(CHUNKS):
        to_core(i, y).wait_recv()
        to_y(i).wait_recv()
        out[:, i * step : (i + 1) * step] = (
            part[i, k].astype(f32) + cbuf[i, y].astype(f32) + yrecv[i].astype(f32)
        ).astype(bf16)
    for i in range(CHUNKS):
        to_y(i).wait_send()
        to_core(i, 1 - y).wait_send()
        to_core(i, y).wait_send()

    @pl.loop(1, n)
    def _(d):
        to_all(d).wait_send()


def share(back, w, loss, n):
    rows = back.shape[1] // QUAD
    depth = w.shape[1]
    step = depth // CHUNKS
    dma = pltpu.SemaphoreType.DMA
    vmem = pl.BlockSpec(memory_space=pltpu.VMEM)
    bf16 = jnp.bfloat16
    return pl.pallas_call(
        functools.partial(share_kernel, n),
        out_shape=(
            jax.ShapeDtypeStruct((rows, depth), bf16),
            jax.ShapeDtypeStruct((8, 128), jnp.float32),
        ),
        in_specs=[pl.BlockSpec(memory_space=pl.ANY)] * 3,
        out_specs=(vmem, vmem),
        scratch_shapes=[
            pltpu.VMEM(back.shape, bf16),
            pltpu.VMEM(w.shape, bf16),
            pltpu.VMEM((CHUNKS, QUAD, rows, step), bf16),
            pltpu.VMEM((CHUNKS, 2, rows, step), bf16),
            pltpu.VMEM((CHUNKS, rows, step), bf16),
            pltpu.VMEM((CHUNKS, rows, step), bf16),
            pltpu.VMEM((n, 8, 128), jnp.float32),
            dma((CHUNKS,)), dma((2,)), dma((CHUNKS, 2)), dma((CHUNKS, 2)), dma((CHUNKS,)), dma((CHUNKS,)),
            dma((n,)), dma((n,)),
        ],
        compiler_params=pltpu.CompilerParams(
            collective_id=1, has_side_effects=True, vmem_limit_bytes=58 * 1024 * 1024),
    )(back, w, loss)


def per_device(
    tokens, target, w_query, w_key, w_value, q_gain, k_gain, block_weight, block_reset, valid_count
):
    rows, width = tokens.shape
    n = lax.axis_size("tm")
    block = 2 * rows
    tok, tgt, w = gather(tokens, target, w_query, w_key, w_value, n)
    w = w.reshape(3, width, -1)
    back, loss = layer(
        valid_count,
        block_reset,
        block_weight,
        tok.reshape(8 * rows, width),
        tgt.reshape(6 * rows, -1),
        w,
        q_gain,
        k_gain,
        block,
    )
    grad, loss_sum = share(back, w, loss, n)
    size = rows * n * w_query.shape[1]
    return grad, (loss_sum[0, :1] / size).reshape(1)


def solution(mesh):
    return jax.shard_map(
        per_device,
        mesh=mesh,
        in_specs=(
            P(("groups", "tm"), None),
            P(("groups", "tm"), None),
            P("tm", None),
            P("tm", None),
            P("tm", None),
            P(),
            P(),
            P("groups"),
            P("groups"),
            P("groups"),
        ),
        out_specs=(P(("groups", "tm"), None), P("groups")),
        check_vma=False,
    )
```
